32 devices in a mesh: fsdp: 8 (over z, y), grp: 4 (over x, core).
Axes of the slice: x: 2, y: 2, z: 4, core: 2. Of those that a mesh axis runs over, the one named last changes fastest.
Arguments:
- grads: bfloat16 [4, 8, 128, 8192], P('grp', 'fsdp'), may hold values from -6 to 6
- master: float32 [128, 8192], P('fsdp', 'grp'), may hold values from -0.0625 to 0.0625
- moment_one: float32 [128, 8192], P('fsdp', 'grp'), may hold values from -0.2 to 0.2
- moment_two: float32 [128, 8192], P('fsdp', 'grp'), may hold values from 0.0001 to 0.004
Outputs:
- new_master: float32 [128, 8192], P('fsdp', 'grp')
- new_first: float32 [128, 8192], P('fsdp', 'grp')
- new_second: float32 [128, 8192], P('fsdp', 'grp')
- weights: bfloat16 [128, 8192], P('fsdp')
- copy_master: float32 [128, 8192], P('fsdp', 'grp')
- copy_first: float32 [128, 8192], P('fsdp', 'grp')
- copy_second: float32 [128, 8192], P('fsdp', 'grp')
The draws below stay inside these ranges and needn't reach their ends.
All inputs are finite; a program needn't handle non-finite values.
Results may differ from the reference program's by a relative error of at most 0.009.
Values may be sent and summed in bfloat16 or wider, within the bound.
No kernel may reach another device: no remote copies, remote signals or barrier semaphores. Data moves between devices by JAX's collectives and lax.ppermute only.
A program may use at most 64 MiB of HBM per device.

```python
import math
import jax
import jax.numpy as jnp
from jax import lax

D = 8192
ROWS = 128
N_FSDP = 8
N_GRP = 4


def with_spikes(values, rng, source, target, blocks, factor):
    owner, partner = [(jnp.arange(values.shape[axis_at]) // (values.shape[axis_at] // blocks)).reshape([-1 if axis == axis_at else 1 for axis in range(values.ndim)]) for axis_at in (source, target)]
    chosen = jax.random.permutation(rng, blocks)[partner]
    strong = (owner == chosen) | (owner == (partner + blocks // 2) % blocks)
    return jnp.where(strong, factor * values, values)


def shard_levels(stream_key, dims, shards, least, high):
    level, own = 1.0, jax.random.fold_in(stream_key, 6)
    for dim, blocks in shards:
        steps = jnp.exp(jax.random.uniform(jax.random.fold_in(own, dim), (blocks,), jnp.float32, least / len(shards), high / len(shards)))
        level = level * jnp.repeat(steps, dims[dim] // blocks).reshape([-1 if axis == dim else 1 for axis in range(len(dims))])
    return level


def bell_draw(key, shape, spread, limit, shards=(), dtype=jnp.bfloat16):
    factor_of = shard_levels(key, shape, shards, -0.22, 0.18) if shards else 1.0
    array = jax.random.normal(key, shape, jnp.float32) * spread * factor_of
    return jnp.minimum(jnp.maximum(array, -limit), limit).astype(dtype)


def noise_with(rng, shape, width, limit, shards, heavy, dtype=jnp.bfloat16):
    entries = width * jax.random.normal(rng, shape, jnp.float32)
    if shards:
        entries = entries * shard_levels(rng, shape, shards, -0.22, 0.18)
    return jnp.clip(with_spikes(entries, jax.random.fold_in(rng, 3), *heavy), -limit, limit).astype(dtype)


def setup_inputs(seed: int = 0) -> dict:
    keys = jax.random.split(jax.random.key(seed), 5)
    return {
        "grads": noise_with(keys[0], (N_GRP, N_FSDP, ROWS, D), 1.0, 6.0, ((0, 4), (1, 8)), (1, 2, 8, 2.0)),
        "master": bell_draw(keys[1], (ROWS, D), D ** -0.5, 0.0625, ((0, 8), (1, 4)), jnp.float32),
        "moment_one": bell_draw(keys[2], (ROWS, D), 0.03, 0.2, ((0, 8), (1, 4)), jnp.float32),
        "moment_two": jnp.clip(jnp.exp(math.log(0.004) - 3.6888795 * jax.random.uniform(keys[3], (ROWS, D), jnp.float32) ** shard_levels(keys[3], (ROWS, D), ((0, 8), (1, 4)), -0.2, 0.2)), 0.0001, 0.004),
    }


beta_one = 0.9
beta_two = 0.95
learn_rate = 0.01
decay_rate = 0.1
epsilon = 1e-08
step_count = 100

def accumulate(carry, block):
    return (carry + lax.optimization_barrier(jnp.sum(block.astype(jnp.float32), axis=0)), None)

def reference(grads, master, moment_one, moment_two):
    summed, _ = lax.scan(accumulate, jnp.zeros((ROWS, D), jnp.float32), grads)
    gradient = summed / (N_GRP * N_FSDP)
    new_first = beta_one * moment_one + (1.0 - beta_one) * gradient
    new_second = beta_two * moment_two + (1.0 - beta_two) * gradient * gradient
    first_hat = new_first / (1.0 - beta_one ** step_count)
    second_hat = new_second / (1.0 - beta_two ** step_count)
    new_master = master - learn_rate * (first_hat / (jnp.sqrt(second_hat) + epsilon) + decay_rate * master)
    weights = new_master.astype(jnp.bfloat16)
    offset = D // N_GRP
    copy_master = jnp.roll(new_master, offset, axis=1)
    copy_first = jnp.roll(new_first, offset, axis=1)
    copy_second = jnp.roll(new_second, offset, axis=1)
    return (new_master, new_first, new_second, weights, copy_master, copy_first, copy_second)
```

```python
import jax
import jax.numpy as jnp
from jax import lax
from jax.sharding import PartitionSpec as P

beta_one = 0.9
beta_two = 0.95
learn_rate = 0.01
decay_rate = 0.1
epsilon = 1e-08
step_count = 100
F32 = jnp.float32
BF16 = jnp.bfloat16


def swap(x, axis, mask):
    n = lax.axis_size(axis)
    return lax.ppermute(x, axis, [(i, i ^ mask) for i in range(n)])


def pick(t, index, dim):
    return lax.dynamic_index_in_dim(t, index, dim, keepdims=False)


def halve(t, dims, step):
    axis, bit = step
    mine = (lax.axis_index(axis) >> bit) & 1
    dim = dims.index(step)
    got = swap(pick(t, 1 - mine, dim).astype(BF16), axis, 1 << bit)
    kept = pick(t, mine, dim).astype(F32) + got.astype(F32)
    return kept, dims[:dim] + dims[dim + 1 :]


def shards(grads, master, moment_one, moment_two):
    g = grads[0, 0]
    ng, nf = lax.axis_size("grp"), lax.axis_size("fsdp")
    me_g, me_f = lax.axis_index("grp"), lax.axis_index("fsdp")
    rows, cols = g.shape[0] // nf, g.shape[1] // ng
    g_steps = [("grp", b) for b in range(1, ng.bit_length() - 1)]
    f_steps = [("fsdp", b) for b in range(nf.bit_length() - 1)]
    dims0 = g_steps[::-1] + f_steps[::-1]
    core = me_g & 1
    g_core = g
    portions = []
    start = 0
    cuts = [('gf', 8), ('fg', 8)]
    for order, share in cuts:
        width = cols * share // 16
        sides = []
        for side in (1 - core, core):
            part = [lax.dynamic_slice(g, (0, (2 * k + side) * cols + start), (g.shape[0], width)) for k in range(ng // 2)]
            sides.append(jnp.stack(part).reshape((2,) * len(dims0) + (rows, width)))
        start += width
        portions.append([sides[0], sides[1], order, dims0])
    for p in portions:
        p[0] = swap(p[0], "grp", 1)
    state = []
    for got, own, order, dims in portions:
        t = own.astype(F32) + got.astype(F32)
        steps = {"gf": g_steps + f_steps, "fg": f_steps + g_steps, "yxz": f_steps[:1] + g_steps + f_steps[1:], "zxy": f_steps[1:] + g_steps + f_steps[:1], "zyx": f_steps[1:] + f_steps[:1] + g_steps}[order]
        state.append((t, dims, steps))
    for k in range(len(dims0)):
        state = [halve(t, dims, steps[k]) + (steps,) for t, dims, steps in state]
    gradient = jnp.concatenate([t for t, _, _ in state], 1) / (ng * nf)
    new_first = beta_one * moment_one + (1.0 - beta_one) * gradient
    new_second = beta_two * moment_two + (1.0 - beta_two) * gradient * gradient
    first_hat = new_first / (1.0 - beta_one**step_count)
    second_hat = new_second / (1.0 - beta_two**step_count)
    new_master = master - learn_rate * (
        first_hat / (jnp.sqrt(second_hat) + epsilon) + decay_rate * master
    )
    w = new_master.astype(BF16)

    pack = jnp.stack([w, new_first.astype(BF16), new_second.astype(BF16)])
    weights = jnp.zeros((rows, cols * ng), BF16)
    weights = lax.dynamic_update_slice(weights, w, (0, me_g * cols))
    got = {}
    for k in range(1, ng):
        got[k] = lax.ppermute(pack if k == 1 else w, "grp", [(i, (i + k) % ng) for i in range(ng)])
    copy_master, copy_first, copy_second = got[1].astype(F32)
    for k in range(1, ng):
        weights = lax.dynamic_update_slice(weights, got[k][0] if k == 1 else got[k], (0, ((me_g + ng - k) % ng) * cols))

    return (new_master, new_first, new_second, weights, copy_master, copy_first, copy_second)


def solution(mesh):
    return jax.shard_map(
        shards,
        mesh=mesh,
        in_specs=(P("grp", "fsdp", None, None), P("fsdp", "grp"), P("fsdp", "grp"), P("fsdp", "grp")),
        out_specs=(P("fsdp", "grp"), P("fsdp", "grp"), P("fsdp", "grp"), P("fsdp", None), P("fsdp", "grp"), P("fsdp", "grp"), P("fsdp", "grp")),
        check_vma=False,
    )
```

```python
import jax
import jax.numpy as jnp
from jax import lax
from jax.experimental import pallas as pl
from jax.experimental.pallas import tpu as pltpu
from jax.sharding import PartitionSpec as P

beta_one = 0.9
beta_two = 0.95
learn_rate = 0.01
decay_rate = 0.1
epsilon = 1e-08
step_count = 100
F32 = jnp.float32
BF16 = jnp.bfloat16
BOTH = ("fsdp", "grp")
LIMIT = 4 * 2**20
SPLITS = [2]
VMEM = pl.BlockSpec(memory_space=pltpu.VMEM)
ANY = pl.BlockSpec(memory_space=pl.ANY)


def device_bit(bit, n_grp):
    flat = lax.axis_index("fsdp") * n_grp + lax.axis_index("grp")
    return (flat >> bit) & 1


def swap(x, masks):
    n = lax.axis_size("fsdp") * lax.axis_size("grp")
    return lax.ppermute(x, BOTH, [(i, i ^ masks[i & 1]) for i in range(n)])


def pick(t, index, dim):
    return lax.dynamic_index_in_dim(t, index, dim, keepdims=False)


def updated(gradient, master, moment_one, moment_two):
    new_first = beta_one * moment_one + (1.0 - beta_one) * gradient
    new_second = beta_two * moment_two + (1.0 - beta_two) * gradient * gradient
    first_hat = new_first / (1.0 - beta_one**step_count)
    second_hat = new_second / (1.0 - beta_two**step_count)
    new_master = master - learn_rate * (
        first_hat / (jnp.sqrt(second_hat) + epsilon) + decay_rate * master
    )
    return new_master, new_first, new_second


def widths(cols, parts):
    cuts = [cols * k // parts // 128 * 128 for k in range(parts)] + [cols]
    return [b - a for a, b in zip(cuts, cuts[1:])]


def shards(grads, master, moment_one, moment_two):
    ng, nf = lax.axis_size("grp"), lax.axis_size("fsdp")
    g_bits, f_bits = ng.bit_length() - 1, nf.bit_length() - 1
    me_g = lax.axis_index("grp")
    g = grads[0, 0]
    rows, cols = g.shape[0] // nf, g.shape[1] // ng
    bit = [device_bit(k, ng) for k in range(g_bits + f_bits)]
    core, over = bit[0], ng // 4

    def place(core, j, away):
        return jnp.where(core == 0, bit[1] ^ away, j), jnp.where(core == 0, j, bit[g_bits] ^ away)

    def pieces(core, away, start, width):
        rolled = g.reshape((2,) * f_bits + (rows, g.shape[1]))
        halves = []
        for j in range(2):
            x, y = place(core, j, away)
            half = pick(rolled, y, f_bits - 1)
            sides = [lax.dynamic_slice_in_dim(half, (4 * k + 2 * x + core) * cols + start, width, f_bits) for k in range(over)]
            halves.append(jnp.stack(sides))
        return jnp.stack(halves).reshape((2,) * (g_bits - 2 + f_bits) + (rows, width))

    cut = widths(cols, SPLITS[0])
    near = [1, 1]

    starts = [sum(cut[:k]) for k in range(len(cut))]
    if over == 1 and rows % 16 == 0 and min(cut) % 128 == 0:
        away_out, = gathered(g, [(1, 1)], cut, rows, nf)
        kept_out, away_own, kept_own = gathered(g, [(1, 0), (0, 1), (0, 0)], cut, rows, nf)
        shape = (2,) * (g_bits - 2 + f_bits) + (rows,)
        away_out, kept_out, away_own, kept_own = [[t.reshape(shape + t.shape[-1:]) for t in ts] for ts in (away_out, kept_out, away_own, kept_own)]
    else:
        away_out, kept_out, away_own, kept_own = [
            [pieces(c, away, a, w) for a, w in zip(starts, cut)] for c, away in ((1 - core, 1), (1 - core, 0), (core, 1), (core, 0))
        ]
    got_away = [swap(t, near) for t in away_out]
    got_kept = [swap(t, near) for t in kept_out]
    sent = [(t.astype(F32) + x.astype(F32)).astype(BF16) for t, x in zip(away_own, got_away)]
    kept = [t.astype(F32) + x.astype(F32) for t, x in zip(kept_own, got_kept)]

    dims = list(range(g_bits - 1, 1, -1)) + list(range(g_bits + f_bits - 1, g_bits, -1))
    pair = (1, g_bits)
    left = list(range(2, g_bits)) + list(range(g_bits + 1, g_bits + f_bits))
    step = 0
    while True:
        p, q = pair
        got = [swap(s, [1 << p, 1 << q]) for s in sent]
        ts = [k + x.astype(F32) for k, x in zip(kept, got)]
        step += 1
        ts = recut(ts, cols, SPLITS[min(step, len(SPLITS) - 1)])
        if p != q:
            mine = jnp.where(core == 0, bit[q], bit[p])
            got = [swap(pick(t, 1 - mine, 0).astype(BF16), [1 << q, 1 << p]) for t in ts]
            ts = [pick(t, mine, 0) + x.astype(F32) for t, x in zip(ts, got)]
            step += 1
            ts = recut(ts, cols, SPLITS[min(step, len(SPLITS) - 1)])
        if not left:
            break
        pair = (left[0], left[1]) if len(left) > 1 else (left[0], left[0])
        left = left[2:]
        p, q = pair
        at_p, at_q = dims.index(p), dims.index(q)

        def choose(t, j, away):
            i_p = jnp.where(core == 0, bit[p] ^ away, j)
            i_q = jnp.where(core == 0, j, bit[q] ^ away)
            first, last = ((i_p, at_p), (i_q, at_q)) if at_p > at_q else ((i_q, at_q), (i_p, at_p))
            return pick(pick(t, *first), *last)

        if p == q:
            sent = [pick(t, 1 - bit[p], at_p).astype(BF16) for t in ts]
            kept = [pick(t, bit[p], at_p) for t in ts]
        else:
            sent = [jnp.stack([choose(t, j, 1) for j in range(2)]).astype(BF16) for t in ts]
            kept = [jnp.stack([choose(t, j, 0) for j in range(2)]) for t in ts]
        dims = [d for d in dims if d not in pair]
    gradient = recut(ts, cols, 1)[0] / (ng * nf)

    early = updated(gradient, master, moment_one, moment_two)
    pack = lax.optimization_barrier(jnp.stack([e.astype(BF16) for e in early]))
    w = pack[0]
    new_master, new_first, new_second = updated(*lax.optimization_barrier((gradient, master, moment_one, moment_two)))
    got = [pack]
    for k in range(1, ng):
        got.append(lax.ppermute(pack if k == 1 else w, "grp", [(i, (i + k) % ng) for i in range(ng)]))
    if rows % 16 == 0 and cols % 128 == 0:
        weights, copy_master, copy_first, copy_second = spread(got)
    else:
        weights = jnp.zeros((rows, cols * ng), BF16)
        for k in range(ng):
            weights = lax.dynamic_update_slice(weights, got[k][0] if k < 2 else got[k], (0, ((me_g + ng - k) % ng) * cols))
        copy_master, copy_first, copy_second = got[1].astype(F32)

    return (new_master, new_first, new_second, weights, copy_master, copy_first, copy_second)


def recut(ts, cols, parts):
    if len(ts) == parts:
        return ts
    whole = jnp.concatenate(ts, -1) if len(ts) > 1 else ts[0]
    starts = [sum(widths(cols, parts)[:k]) for k in range(parts + 1)]
    return [lax.slice_in_dim(whole, a, b, axis=whole.ndim - 1) for a, b in zip(starts, starts[1:])] if parts > 1 else [whole]


def gathered(g, wanted, cut, rows, nf):
    cols = sum(cut)
    starts = [sum(cut[:k]) for k in range(len(cut))]

    def kernel(g_ref, *refs):
        outs, sem = refs[:-1], refs[-1]
        me_f, me_g = lax.axis_index("fsdp"), lax.axis_index("grp")
        copies = []
        for n, (sibling, away) in enumerate(wanted):
            core = (me_g & 1) ^ sibling
            for j in range(2):
                x = jnp.where(core == 0, (me_g >> 1) ^ away, j)
                y = jnp.where(core == 0, j, (me_f & 1) ^ away)
                base = (2 * x + core) * cols
                for k, (a, w) in enumerate(zip(starts, cut)):
                    column = pl.multiple_of(base + a, 128)
                    copies.append(pltpu.make_async_copy(g_ref.at[:, y, :, pl.ds(column, w)], outs[n * len(cut) + k].at[j], sem.at[len(copies)]))
        for c in copies:
            c.start()
        for c in copies:
            c.wait()

    size = g.size * 2 // nf // 4 // 2
    flat = pl.pallas_call(
        kernel,
        out_shape=[jax.ShapeDtypeStruct((2, nf // 2, rows, w), g.dtype) for _ in wanted for w in cut],
        in_specs=[ANY],
        out_specs=[VMEM] * (len(wanted) * len(cut)),
        scratch_shapes=[pltpu.SemaphoreType.DMA((2 * len(wanted) * len(cut),))],
        compiler_params=pltpu.CompilerParams(vmem_limit_bytes=LIMIT),
        cost_estimate=pl.CostEstimate(flops=0, bytes_accessed=g.size * len(wanted), transcendentals=0),
    )(g.reshape(nf // 2, 2, rows, g.shape[1]))
    return [flat[n * len(cut) : (n + 1) * len(cut)] for n in range(len(wanted))]


def spread(got):
    ng, (rows, cols) = len(got), got[2].shape

    def kernel(*refs):
        me = lax.axis_index("grp")
        blocks, weights, copies, wide, sem = refs[:ng], refs[ng], refs[ng + 1 : ng + 4], refs[ng + 4], refs[ng + 5]
        moves = []
        for k in range(ng):
            owner = lax.rem(me + ng - k, ng)
            source = blocks[k].at[0] if k < 2 else blocks[k]
            moves.append(pltpu.make_async_copy(source, weights.at[:, pl.ds(pl.multiple_of(owner * cols, 128), cols)], sem.at[k]))
            moves[-1].start()
        for k in range(3):
            wide[k] = blocks[1][k].astype(F32)
            moves.append(pltpu.make_async_copy(wide.at[k], copies[k], sem.at[ng + k]))
            moves[-1].start()
        for m in moves:
            m.wait()

    return pl.pallas_call(
        kernel,
        out_shape=[jax.ShapeDtypeStruct((rows, cols * ng), BF16)] + [jax.ShapeDtypeStruct((rows, cols), F32)] * 3,
        in_specs=[VMEM] * ng,
        out_specs=[ANY] * 4,
        scratch_shapes=[pltpu.VMEM((3, rows, cols), F32), pltpu.SemaphoreType.DMA((ng + 3,))],
        compiler_params=pltpu.CompilerParams(vmem_limit_bytes=LIMIT),
    )(*got)


def solution(mesh):
    return jax.shard_map(
        shards,
        mesh=mesh,
        in_specs=(P("grp", "fsdp", None, None), P("fsdp", "grp"), P("fsdp", "grp"), P("fsdp", "grp")),
        out_specs=(P("fsdp", "grp"), P("fsdp", "grp"), P("fsdp", "grp"), P("fsdp", None), P("fsdp", "grp"), P("fsdp", "grp"), P("fsdp", "grp")),
        check_vma=False,
    )
```

```python
import jax
import jax.numpy as jnp
from jax import lax
from jax.experimental import pallas as pl
from jax.experimental.pallas import tpu as pltpu
from jax.sharding import PartitionSpec as P

beta_one = 0.9
beta_two = 0.95
learn_rate = 0.01
decay_rate = 0.1
epsilon = 1e-08
step_count = 100
F32 = jnp.float32
BF16 = jnp.bfloat16
BOTH = ("fsdp", "grp")
SHARES = [1, 1]
VMEM = pl.BlockSpec(memory_space=pltpu.VMEM)
ANY = pl.BlockSpec(memory_space=pl.ANY)
HBM = pl.BlockSpec(memory_space=pltpu.HBM)
LIMIT = 4 * 2**20


def swap(x, masks):
    n = lax.axis_size("fsdp") * lax.axis_size("grp")
    return lax.ppermute(x, BOTH, [(i, i ^ masks[i & 1]) for i in range(n)])


def pick(t, index, axis):
    return lax.dynamic_index_in_dim(t, index, axis, keepdims=False)


def updated(gradient, master, moment_one, moment_two):
    new_first = beta_one * moment_one + (1.0 - beta_one) * gradient
    new_second = beta_two * moment_two + (1.0 - beta_two) * gradient * gradient
    first_hat = new_first / (1.0 - beta_one**step_count)
    second_hat = new_second / (1.0 - beta_two**step_count)
    new_master = master - learn_rate * (
        first_hat / (jnp.sqrt(second_hat) + epsilon) + decay_rate * master
    )
    return new_master, new_first, new_second


def cut_up(cols):
    edges = [cols * sum(SHARES[:k]) // sum(SHARES) // 128 * 128 for k in range(len(SHARES))] + [cols]
    return [(a, b - a) for a, b in zip(edges, edges[1:]) if b > a]


def first_block(core, me_f, j, away):
    low, high = me_f & 1, (me_f >> 1) & 1
    return jnp.where(core == 0, low ^ away, j), jnp.where(core == 0, j, high ^ away)


def gathered(g, wanted, cut, rows, nf, ng):
    cols = g.shape[1] // ng
    blocks = g.reshape(nf // 4, 2, 2, rows, g.shape[1])

    def kernel(g_ref, *refs):
        outs, sem = refs[:-1], refs[-1]
        me_f, me_g = lax.axis_index("fsdp"), lax.axis_index("grp")
        moves = []
        for n, (sibling, away) in enumerate(wanted):
            core = (me_g & 1) ^ sibling
            for k, (start, width) in enumerate(cut):
                for j in range(2):
                    low, high = first_block(core, me_f, j, away)
                    for x in range(ng // 2):
                        column = pl.multiple_of((2 * x + core) * cols + start, 128)
                        moves.append(pltpu.make_async_copy(
                            g_ref.at[:, high, low, :, pl.ds(column, width)], outs[n * len(cut) + k].at[j, :, x], sem.at[len(moves)]))
        for m in moves:
            m.start()
        for m in moves:
            m.wait()

    flat = pl.pallas_call(
        kernel,
        out_shape=[jax.ShapeDtypeStruct((2, nf // 4, ng // 2, rows, w), g.dtype) for _ in wanted for _, w in cut],
        in_specs=[HBM],
        out_specs=[VMEM] * (len(wanted) * len(cut)),
        scratch_shapes=[pltpu.SemaphoreType.DMA((ng * len(wanted) * len(cut),))],
        compiler_params=pltpu.CompilerParams(vmem_limit_bytes=LIMIT),
        cost_estimate=pl.CostEstimate(flops=0, bytes_accessed=g.size * len(wanted), transcendentals=0),
    )(blocks)
    return [flat[n * len(cut) : (n + 1) * len(cut)] for n in range(len(wanted))]


def gathered_plain(g, wanted, cut, rows, nf, ng):
    cols = g.shape[1] // ng
    blocks = g.reshape(nf // 4, 2, 2, rows, g.shape[1])
    me_f, me_g = lax.axis_index("fsdp"), lax.axis_index("grp")

    def block(core, away, j, x, start, width):
        low, high = first_block(core, me_f, j, away)
        part = lax.dynamic_slice(blocks, (0, high, low, 0, (2 * x + core) * cols + start), (nf // 4, 1, 1, rows, width))
        return part[:, 0, 0]

    return [
        [jnp.stack([jnp.stack([block((me_g & 1) ^ sibling, away, j, x, a, w) for x in range(ng // 2)], 1) for j in range(2)]) for a, w in cut]
        for sibling, away in wanted
    ]


def finish(own, other, states, near, cols):
    parts, rows = len(own), own[0].shape[1]
    ng = 2 * len(states)
    edges = cut_up(cols)

    def kernel(*refs):
        refs = list(refs)
        take = lambda n: [refs.pop(0) for _ in range(n)]
        own, other, states, near = take(parts), take(parts), take(ng // 2), take(ng // 2)
        outs, weights, copies = take(3), take(1)[0], take(3)
        wide, thin, sem = take(3)
        me = lax.axis_index("grp")
        last = lax.rem(me + ng - 1, ng)
        moves = []

        def move(source, target):
            moves.append(pltpu.make_async_copy(source, target, sem.at[len(moves)]))
            moves[-1].start()

        order = [(0, 0)] + [(k, odd) for odd in (0, 1) for k in range(ng // 2) if k or odd]
        for n, (k, odd) in enumerate(order):
            x = (me >> 1) ^ k
            owner = me ^ (2 * k + odd)
            state = near[k] if odd else states[k]
            for part, (a, w) in zip(other if odd else own, edges):
                new = updated(part[x], *[state[i, :, a : a + w] for i in range(3)])
                thin[n, :, a : a + w] = new[0].astype(BF16)
                if n == 0:
                    for i in range(3):
                        wide[i, :, a : a + w] = new[i]
            if n == 0:
                for i in range(3):
                    move(wide.at[i], outs[i])
            move(thin.at[n], weights.at[:, pl.ds(pl.multiple_of(owner * cols, 128), cols)])
        for k in range(ng // 2):
            @pl.when((me ^ last) >> 1 == k)
            def _():
                for part, (a, w) in zip(other, edges):
                    new = updated(part[last >> 1], *[near[k][i, :, a : a + w] for i in range(3)])
                    for i in range(3):
                        wide[3 + i, :, a : a + w] = new[i]
        for i in range(3):
            move(wide.at[3 + i], copies[i])
        for m in moves:
            m.wait()

    shape = jax.ShapeDtypeStruct((rows, cols), F32)
    return pl.pallas_call(
        kernel,
        out_shape=[shape] * 3 + [jax.ShapeDtypeStruct((rows, cols * ng), BF16)] + [shape] * 3,
        in_specs=[VMEM] * (2 * parts + ng),
        out_specs=[ANY] * 7,
        scratch_shapes=[pltpu.VMEM((6, rows, cols), F32), pltpu.VMEM((ng, rows, cols), BF16), pltpu.SemaphoreType.DMA((ng + 6,))],
        compiler_params=pltpu.CompilerParams(vmem_limit_bytes=LIMIT),
    )(*own, *other, *states, *near)


def finish_plain(own, other, states, near, cols):
    me = lax.axis_index("grp")
    own, other = jnp.concatenate(own, -1), jnp.concatenate(other, -1)
    ng = 2 * len(states)
    weights = jnp.zeros((own.shape[1], cols * ng), BF16)
    last = (me + ng - 1) % ng
    for k in range(ng // 2):
        for odd, grad, state in ((0, own, states[k]), (1, other, near[k])):
            new = updated(pick(grad, (me >> 1) ^ k, 0), *state)
            owner = me ^ (2 * k + odd)
            weights = lax.dynamic_update_slice(weights, new[0].astype(BF16), (0, owner * cols))
            if k == 0 and odd == 0:
                mine = new
            if odd:
                copies = new if k == 0 else [jnp.where(owner == last, a, b) for a, b in zip(new, copies)]
    return (*mine, weights, *copies)


def shards(grads, master, moment_one, moment_two):
    ng, nf = lax.axis_size("grp"), lax.axis_size("fsdp")
    g_bits, f_bits = ng.bit_length() - 1, nf.bit_length() - 1
    me_f, me_g = lax.axis_index("fsdp"), lax.axis_index("grp")
    core = me_g & 1
    g = grads[0, 0]
    rows, cols = g.shape[0] // nf, g.shape[1] // ng
    cut = cut_up(cols)
    local = rows % 16 == 0 and cols % 128 == 0

    gather = gathered if local else gathered_plain
    (away_out,) = gather(g, [(1, 1)], cut, rows, nf, ng)
    kept_out, away_own, kept_own = gather(g, [(1, 0), (0, 1), (0, 0)], cut, rows, nf, ng)
    split = lambda t: t.reshape((2,) * (f_bits - 1) + t.shape[2:])
    got_away = [split(swap(t, [1, 1])) for t in away_out]
    got_kept = [split(swap(t, [1, 1])) for t in kept_out]
    sent = [(split(t).astype(F32) + x.astype(F32)).astype(BF16) for t, x in zip(away_own, got_away)]
    kept = [split(t).astype(F32) + x.astype(F32) for t, x in zip(kept_own, got_kept)]

    high = list(range(f_bits - 1, 1, -1))
    labels = [[1] + high, [0] + high]
    orders = [[0, 1, 2], [1, 2, 0]]
    orders = [o + [b for b in range(f_bits) if b not in o] for o in orders]
    for step in range(f_bits):
        masks = [ng << o[step] for o in orders]
        if step == 0:
            sent[-1], held = lax.optimization_barrier((sent[-1], (master, moment_one, moment_two)))
            states = [jnp.stack(held)]
            for b in range(1, g_bits):
                states = states + [swap(s, [1 << b] * 2) for s in states]
        got = [swap(s, masks) for s in sent]

        ts = [k + x.astype(F32) for k, x in zip(kept, got)]
        if step == f_bits - 1:
            break
        want = [o[step + 1] for o in orders]
        a, b = [l.index(w) for l, w in zip(labels, want)]
        bit = [(me_f >> w) & 1 for w in want]

        def choose(t, j, away):
            if a == b:
                return pick(t, jnp.where(core == 0, bit[0], bit[1]) ^ away, a)
            at = {a: jnp.where(core == 0, bit[0] ^ away, j), b: jnp.where(core == 0, j, bit[1] ^ away)}
            return pick(pick(t, at[max(a, b)], max(a, b)), at[min(a, b)], min(a, b))

        def chosen(t, away):
            return choose(t, 0, away) if a == b else jnp.stack([choose(t, j, away) for j in range(2)])

        sent = [chosen(t, 1).astype(BF16) for t in ts]
        kept = [chosen(t, 0) for t in ts]
        rest = [[x for i, x in enumerate(l) if i not in (a, b)] for l in labels]
        labels = rest if a == b else [[labels[0][b]] + rest[0], [labels[1][a]] + rest[1]]

    for b in range(1, g_bits):
        rounded = [t.astype(BF16) for t in ts]
        if b == g_bits - 1:
            rounded, states = lax.optimization_barrier((rounded, states))
            near = [swap(s, [1, 1]) for s in states]

        got = [swap(t, [1 << b] * 2) for t in rounded]
        ts = [t.astype(F32) + x.astype(F32) for t, x in zip(rounded, got)]
    own = [t / (ng * nf) for t in ts]
    other = [swap(t, [1, 1]) for t in own]
    return (finish if local else finish_plain)(own, other, states, near, cols)


def solution(mesh):
    return jax.shard_map(
        shards,
        mesh=mesh,
        in_specs=(P("grp", "fsdp", None, None), P("fsdp", "grp"), P("fsdp", "grp"), P("fsdp", "grp")),
        out_specs=(P("fsdp", "grp"), P("fsdp", "grp"), P("fsdp", "grp"), P("fsdp", None), P("fsdp", "grp"), P("fsdp", "grp"), P("fsdp", "grp")),
        check_vma=False,
    )
```

```python
import jax
import jax.numpy as jnp
from jax import lax
from jax.experimental import pallas as pl
from jax.experimental.pallas import tpu as pltpu
from jax.sharding import PartitionSpec as P

beta_one = 0.9
beta_two = 0.95
learn_rate = 0.01
decay_rate = 0.1
epsilon = 1e-08
step_count = 100
F32 = jnp.float32
BF16 = jnp.bfloat16
BOTH = ("fsdp", "grp")
SHARES = [1, 1]
VMEM = pl.BlockSpec(memory_space=pltpu.VMEM)
ANY = pl.BlockSpec(memory_space=pl.ANY)
HBM = pl.BlockSpec(memory_space=pltpu.HBM)
GLIMIT = 32 * 2**17
LIMIT = 4 * 2**20


def swap(x, masks):
    n = lax.axis_size("fsdp") * lax.axis_size("grp")
    return lax.ppermute(x, BOTH, [(i, i ^ masks[i & 1]) for i in range(n)])


def pick(t, index, axis):
    return lax.dynamic_index_in_dim(t, index, axis, keepdims=False)


def updated(gradient, master, moment_one, moment_two):
    new_first = beta_one * moment_one + (1.0 - beta_one) * gradient
    new_second = beta_two * moment_two + (1.0 - beta_two) * gradient * gradient
    first_hat = new_first / (1.0 - beta_one**step_count)
    second_hat = new_second / (1.0 - beta_two**step_count)
    new_master = master - learn_rate * (
        first_hat / (jnp.sqrt(second_hat) + epsilon) + decay_rate * master
    )
    return new_master, new_first, new_second


def cut_up(cols):
    edges = [cols * sum(SHARES[:k]) // sum(SHARES) // 128 * 128 for k in range(len(SHARES))] + [cols]
    return [(a, b - a) for a, b in zip(edges, edges[1:]) if b > a]


def first_block(core, me_f, j, away):
    low, high = me_f & 1, (me_f >> 1) & 1
    return jnp.where(core == 0, low ^ away, j), jnp.where(core == 0, j, high ^ away)


def gathered(g, wanted, cut, rows, nf, ng):
    cols = g.shape[1] // ng
    blocks = g.reshape(nf // 4, 2, 2, rows, g.shape[1])

    def kernel(g_ref, *refs):
        outs, sem = refs[:-1], refs[-1]
        me_f, me_g = lax.axis_index("fsdp"), lax.axis_index("grp")
        moves = []
        for n, (sibling, away) in enumerate(wanted):
            core = (me_g & 1) ^ sibling
            for k, (start, width) in enumerate(cut):
                for j in range(2):
                    low, high = first_block(core, me_f, j, away)
                    for x in range(ng // 2):
                        column = pl.multiple_of((2 * x + core) * cols + start, 128)
                        moves.append(pltpu.make_async_copy(
                            g_ref.at[:, high, low, :, pl.ds(column, width)], outs[n * len(cut) + k].at[j, :, x], sem.at[len(moves)]))
        for m in moves:
            m.start()
        for m in moves:
            m.wait()

    flat = pl.pallas_call(
        kernel,
        out_shape=[jax.ShapeDtypeStruct((2, nf // 4, ng // 2, rows, w), g.dtype) for _ in wanted for _, w in cut],
        in_specs=[HBM],
        out_specs=[VMEM] * (len(wanted) * len(cut)),
        scratch_shapes=[pltpu.SemaphoreType.DMA((ng * len(wanted) * len(cut),))],
        compiler_params=pltpu.CompilerParams(vmem_limit_bytes=GLIMIT),
        cost_estimate=pl.CostEstimate(flops=0, bytes_accessed=g.size * len(wanted), transcendentals=0),
    )(blocks)
    return [flat[n * len(cut) : (n + 1) * len(cut)] for n in range(len(wanted))]


def gathered_plain(g, wanted, cut, rows, nf, ng):
    cols = g.shape[1] // ng
    blocks = g.reshape(nf // 4, 2, 2, rows, g.shape[1])
    me_f, me_g = lax.axis_index("fsdp"), lax.axis_index("grp")

    def block(core, away, j, x, start, width):
        low, high = first_block(core, me_f, j, away)
        part = lax.dynamic_slice(blocks, (0, high, low, 0, (2 * x + core) * cols + start), (nf // 4, 1, 1, rows, width))
        return part[:, 0, 0]

    return [
        [jnp.stack([jnp.stack([block((me_g & 1) ^ sibling, away, j, x, a, w) for x in range(ng // 2)], 1) for j in range(2)]) for a, w in cut]
        for sibling, away in wanted
    ]


def finish(own, other, states, near, cols):
    parts, rows = len(own), own[0].shape[1]
    ng = 2 * len(states)
    edges = cut_up(cols)

    def kernel(*refs):
        refs = list(refs)
        take = lambda n: [refs.pop(0) for _ in range(n)]
        own, other, states, near = take(parts), take(parts), take(ng // 2), take(ng // 2)
        outs, weights, copies = take(3), take(1)[0], take(3)
        wide, thin, sem = take(3)
        me = lax.axis_index("grp")
        last = lax.rem(me + ng - 1, ng)
        moves = []

        def move(source, target):
            moves.append(pltpu.make_async_copy(source, target, sem.at[len(moves)]))
            moves[-1].start()

        order = [(0, 0)] + [(k, odd) for odd in (0, 1) for k in range(ng // 2) if k or odd]
        for n, (k, odd) in enumerate(order):
            x = (me >> 1) ^ k
            owner = me ^ (2 * k + odd)
            state = near[k] if odd else states[k]
            for part, (a, w) in zip(other if odd else own, edges):
                new = updated(part[x], *[state[i, :, a : a + w] for i in range(3)])
                thin[n, :, a : a + w] = new[0].astype(BF16)
                if n == 0:
                    for i in range(3):
                        wide[i, :, a : a + w] = new[i]
            if n == 0:
                for i in range(3):
                    move(wide.at[i], outs[i])
            move(thin.at[n], weights.at[:, pl.ds(pl.multiple_of(owner * cols, 128), cols)])
        for k in range(ng // 2):
            @pl.when((me ^ last) >> 1 == k)
            def _():
                for part, (a, w) in zip(other, edges):
                    new = updated(part[last >> 1], *[near[k][i, :, a : a + w] for i in range(3)])
                    for i in range(3):
                        wide[3 + i, :, a : a + w] = new[i]
        for i in range(3):
            move(wide.at[3 + i], copies[i])
        for m in moves:
            m.wait()

    shape = jax.ShapeDtypeStruct((rows, cols), F32)
    return pl.pallas_call(
        kernel,
        out_shape=[shape] * 3 + [jax.ShapeDtypeStruct((rows, cols * ng), BF16)] + [shape] * 3,
        in_specs=[VMEM] * (2 * parts + ng),
        out_specs=[ANY] * 7,
        scratch_shapes=[pltpu.VMEM((6, rows, cols), F32), pltpu.VMEM((ng, rows, cols), BF16), pltpu.SemaphoreType.DMA((ng + 6,))],
        compiler_params=pltpu.CompilerParams(vmem_limit_bytes=LIMIT),
    )(*own, *other, *states, *near)


def finish_plain(own, other, states, near, cols):
    me = lax.axis_index("grp")
    own, other = jnp.concatenate(own, -1), jnp.concatenate(other, -1)
    ng = 2 * len(states)
    weights = jnp.zeros((own.shape[1], cols * ng), BF16)
    last = (me + ng - 1) % ng
    for k in range(ng // 2):
        for odd, grad, state in ((0, own, states[k]), (1, other, near[k])):
            new = updated(pick(grad, (me >> 1) ^ k, 0), *state)
            owner = me ^ (2 * k + odd)
            weights = lax.dynamic_update_slice(weights, new[0].astype(BF16), (0, owner * cols))
            if k == 0 and odd == 0:
                mine = new
            if odd:
                copies = new if k == 0 else [jnp.where(owner == last, a, b) for a, b in zip(new, copies)]
    return (*mine, weights, *copies)


def shards(grads, master, moment_one, moment_two):
    ng, nf = lax.axis_size("grp"), lax.axis_size("fsdp")
    g_bits, f_bits = ng.bit_length() - 1, nf.bit_length() - 1
    me_f, me_g = lax.axis_index("fsdp"), lax.axis_index("grp")
    core = me_g & 1
    g = grads[0, 0]
    rows, cols = g.shape[0] // nf, g.shape[1] // ng
    cut = cut_up(cols)
    local = rows % 16 == 0 and cols % 128 == 0

    gather = gathered if local else gathered_plain
    (away_out,) = gather(g, [(1, 1)], cut, rows, nf, ng)
    kept_out, away_own, kept_own = gather(g, [(1, 0), (0, 1), (0, 0)], cut, rows, nf, ng)
    split = lambda t: t.reshape((2,) * (f_bits - 1) + t.shape[2:])
    got_away = [split(swap(t, [1, 1])) for t in away_out]
    got_kept = [split(swap(t, [1, 1])) for t in kept_out]
    sent = [(split(t).astype(F32) + x.astype(F32)).astype(BF16) for t, x in zip(away_own, got_away)]
    kept = [split(t).astype(F32) + x.astype(F32) for t, x in zip(kept_own, got_kept)]

    high = list(range(f_bits - 1, 1, -1))
    labels = [[1] + high, [0] + high]
    orders = [[0, 1, 2], [1, 2, 0]]
    orders = [o + [b for b in range(f_bits) if b not in o] for o in orders]
    for step in range(f_bits):
        masks = [ng << o[step] for o in orders]
        if step == 0:
            sent[-1], held = lax.optimization_barrier((sent[-1], (master, moment_one, moment_two)))
            states = [jnp.stack(held)]
            for b in range(1, g_bits):
                states = states + [swap(s, [1 << b] * 2) for s in states]
        got = [swap(s, masks) for s in sent]

        ts = [k + x.astype(F32) for k, x in zip(kept, got)]
        if step == f_bits - 1:
            break
        want = [o[step + 1] for o in orders]
        a, b = [l.index(w) for l, w in zip(labels, want)]
        bit = [(me_f >> w) & 1 for w in want]

        def choose(t, j, away):
            if a == b:
                return pick(t, jnp.where(core == 0, bit[0], bit[1]) ^ away, a)
            at = {a: jnp.where(core == 0, bit[0] ^ away, j), b: jnp.where(core == 0, j, bit[1] ^ away)}
            return pick(pick(t, at[max(a, b)], max(a, b)), at[min(a, b)], min(a, b))

        def chosen(t, away):
            return choose(t, 0, away) if a == b else jnp.stack([choose(t, j, away) for j in range(2)])

        sent = [chosen(t, 1).astype(BF16) for t in ts]
        kept = [chosen(t, 0) for t in ts]
        rest = [[x for i, x in enumerate(l) if i not in (a, b)] for l in labels]
        labels = rest if a == b else [[labels[0][b]] + rest[0], [labels[1][a]] + rest[1]]

    for b in range(1, g_bits):
        rounded = [t.astype(BF16) for t in ts]
        if b == g_bits - 1:
            rounded[-1], states = lax.optimization_barrier((rounded[-1], states))
            near = [swap(s, [1, 1]) for s in states]

        got = [swap(t, [1 << b] * 2) for t in rounded]
        ts = [t.astype(F32) + x.astype(F32) for t, x in zip(rounded, got)]
    own = [t / (ng * nf) for t in ts]
    other = [swap(t, [1, 1]) for t in own]
    return (finish if local else finish_plain)(own, other, states, near, cols)


def solution(mesh):
    return jax.shard_map(
        shards,
        mesh=mesh,
        in_specs=(P("grp", "fsdp", None, None), P("fsdp", "grp"), P("fsdp", "grp"), P("fsdp", "grp")),
        out_specs=(P("fsdp", "grp"), P("fsdp", "grp"), P("fsdp", "grp"), P("fsdp", None), P("fsdp", "grp"), P("fsdp", "grp"), P("fsdp", "grp")),
        check_vma=False,
    )
```

```python
import functools

import jax
import jax.numpy as jnp
from jax import lax
from jax.experimental import pallas as pl
from jax.experimental.pallas import tpu as pltpu
from jax.sharding import PartitionSpec as P

beta_one = 0.9
beta_two = 0.95
learn_rate = 0.01
decay_rate = 0.1
epsilon = 1e-08
step_count = 100
F32 = jnp.float32
BF16 = jnp.bfloat16
BOTH = ("fsdp", "grp")
SHARES = [1, 1]
ROLES = 0
VMEM = pl.BlockSpec(memory_space=pltpu.VMEM)
ANY = pl.BlockSpec(memory_space=pl.ANY)
HBM = pl.BlockSpec(memory_space=pltpu.HBM)
GLIMIT = 32 * 2**17
LIMIT = 4 * 2**20


def swap(x, masks):
    n = lax.axis_size("fsdp") * lax.axis_size("grp")
    return lax.ppermute(x, BOTH, [(i, i ^ masks[i & 1]) for i in range(n)])


def pick(t, index, axis):
    return lax.dynamic_index_in_dim(t, index, axis, keepdims=False)


def updated(gradient, master, moment_one, moment_two):
    new_first = beta_one * moment_one + (1.0 - beta_one) * gradient
    new_second = beta_two * moment_two + (1.0 - beta_two) * gradient * gradient
    first_hat = new_first / (1.0 - beta_one**step_count)
    second_hat = new_second / (1.0 - beta_two**step_count)
    new_master = master - learn_rate * (
        first_hat / (jnp.sqrt(second_hat) + epsilon) + decay_rate * master
    )
    return new_master, new_first, new_second


def cut_up(cols):
    edges = [cols * sum(SHARES[:k]) // sum(SHARES) // 128 * 128 for k in range(len(SHARES))] + [cols]
    return [(a, b - a) for a, b in zip(edges, edges[1:]) if b > a]


def first_block(core, me_f, j, away):
    low, high = me_f & 1, (me_f >> 1) & 1
    return jnp.where(core == 0, low ^ away, j), jnp.where(core == 0, j, high ^ away)


def role(k):
    return ROLES * (k % 2)


def gathered(g, wanted, cut, rows, nf, ng, limit):
    cols = g.shape[1] // ng
    blocks = g.reshape(nf // 4, 2, 2, rows, g.shape[1])

    def kernel(g_ref, *refs):
        outs, sem = refs[:-1], refs[-1]
        me_f, me_g = lax.axis_index("fsdp"), lax.axis_index("grp")
        moves = []
        for n, (sibling, away) in enumerate(wanted):
            core = (me_g & 1) ^ sibling
            for k, (start, width) in enumerate(cut):
                for j in range(2):
                    low, high = first_block(core ^ role(k), me_f, j, away)
                    for x in range(ng // 2):
                        column = pl.multiple_of((2 * x + core) * cols + start, 128)
                        moves.append(pltpu.make_async_copy(
                            g_ref.at[:, high, low, :, pl.ds(column, width)], outs[n * len(cut) + k].at[j, :, x], sem.at[len(moves)]))
        for m in moves:
            m.start()
        for m in moves:
            m.wait()

    flat = pl.pallas_call(
        kernel,
        out_shape=[jax.ShapeDtypeStruct((2, nf // 4, ng // 2, rows, w), g.dtype) for _ in wanted for _, w in cut],
        in_specs=[HBM],
        out_specs=[VMEM] * (len(wanted) * len(cut)),
        scratch_shapes=[pltpu.SemaphoreType.DMA((ng * len(wanted) * len(cut),))],
        compiler_params=pltpu.CompilerParams(vmem_limit_bytes=limit),
        cost_estimate=pl.CostEstimate(flops=0, bytes_accessed=g.size * len(wanted), transcendentals=0),
    )(blocks)
    return [list(flat[n * len(cut) : (n + 1) * len(cut)]) for n in range(len(wanted))]


def gathered_plain(g, wanted, cut, rows, nf, ng, limit):
    cols = g.shape[1] // ng
    blocks = g.reshape(nf // 4, 2, 2, rows, g.shape[1])
    me_f, me_g = lax.axis_index("fsdp"), lax.axis_index("grp")

    def block(core, k, away, j, x, start, width):
        low, high = first_block(core ^ role(k), me_f, j, away)
        part = lax.dynamic_slice(blocks, (0, high, low, 0, (2 * x + core) * cols + start), (nf // 4, 1, 1, rows, width))
        return part[:, 0, 0]

    return [
        [jnp.stack([jnp.stack([block((me_g & 1) ^ sibling, k, away, j, x, a, w) for x in range(ng // 2)], 1) for j in range(2)]) for k, (a, w) in enumerate(cut)]
        for sibling, away in wanted
    ]


def finish(own, other, states, near, cols):
    parts, rows = len(own), own[0].shape[1]
    ng = 2 * len(states)
    edges = cut_up(cols)

    def kernel(first, *refs):
        refs = list(refs)
        take = lambda n: [refs.pop(0) for _ in range(n)]
        own = take(parts) if first else []
        other = dict(zip(range(parts - 1) if first else [parts - 1], take(parts - 1 if first else 1)))
        states, near = take(ng // 2) if first else [], take(ng // 2)
        if first:
            outs = take(3)
        else:
            take(4)
        weights, copies = take(1)[0], take(3)
        wide, thin, sem = take(3)
        me = lax.axis_index("grp")
        last = lax.rem(me + ng - 1, ng)
        moves = []

        def move(source, target):
            moves.append(pltpu.make_async_copy(source, target, sem.at[len(moves)]))
            moves[-1].start()

        def block(n, part, state, x, edge, keep):
            start, width = edge
            new = updated(part[x], *[state[i, :, start : start + width] for i in range(3)])
            thin[n, :, start : start + width] = new[0].astype(BF16)
            if keep:
                for i in range(3):
                    wide[i, :, start : start + width] = new[i]

        for k in range(len(states)):
            for part, edge in zip(own, edges):
                block(2 * k, part, states[k], (me >> 1) ^ k, edge, k == 0)
            if k == 0:
                for i in range(3):
                    move(wide.at[i], outs[i])
            move(thin.at[2 * k], weights.at[:, pl.ds(pl.multiple_of((me ^ (2 * k)) * cols, 128), cols)])
        for index, part in other.items():
            start, width = edges[index]
            here = pl.ds(start, width)
            for k in range(ng // 2):
                @pl.when((me ^ last) >> 1 == k)
                def _():
                    new = updated(part[last >> 1], *[near[k][i, :, start : start + width] for i in range(3)])
                    for i in range(3):
                        wide[3 + i, :, start : start + width] = new[i]
            for i in range(3):
                move(wide.at[3 + i, :, here], copies[i].at[:, here])
            for k in range(ng // 2):
                block(2 * k + 1, part, near[k], (me >> 1) ^ k, edges[index], False)
                column = pl.multiple_of((me ^ (2 * k + 1)) * cols + start, 128)
                move(thin.at[2 * k + 1, :, here], weights.at[:, pl.ds(column, width)])
        for m in moves:
            m.wait()

    shape = jax.ShapeDtypeStruct((rows, cols), F32)
    shapes = [jax.ShapeDtypeStruct((rows, cols * ng), BF16)] + [shape] * 3
    scratch = [pltpu.VMEM((6, rows, cols), F32), pltpu.VMEM((ng, rows, cols), BF16)]
    early = pl.pallas_call(
        functools.partial(kernel, True),
        out_shape=[shape] * 3 + shapes,
        in_specs=[VMEM] * (2 * parts - 1 + ng),
        out_specs=[ANY] * 7,
        scratch_shapes=scratch + [pltpu.SemaphoreType.DMA((3 + ng // 2 + (3 + ng // 2) * (parts - 1),))],
        cost_estimate=pl.CostEstimate(flops=40 * rows * cols * ng, bytes_accessed=12 * rows * cols * ng, transcendentals=0),
        compiler_params=pltpu.CompilerParams(vmem_limit_bytes=LIMIT),
    )(*own, *other[:-1], *states, *near)
    late = pl.pallas_call(
        functools.partial(kernel, False),
        out_shape=shapes,
        in_specs=[VMEM] * (1 + ng // 2) + [ANY] * 4,
        out_specs=[ANY] * 4,
        scratch_shapes=scratch + [pltpu.SemaphoreType.DMA((3 + ng // 2,))],
        input_output_aliases={1 + ng // 2 + i: i for i in range(4)},
        compiler_params=pltpu.CompilerParams(vmem_limit_bytes=LIMIT),
    )(other[-1], *near, *early[3:])
    return (*early[:3], *late)


def finish_plain(own, other, states, near, cols):
    me = lax.axis_index("grp")
    own, other = jnp.concatenate(own, -1), jnp.concatenate(other, -1)
    ng = 2 * len(states)
    weights = jnp.zeros((own.shape[1], cols * ng), BF16)
    last = (me + ng - 1) % ng
    for k in range(ng // 2):
        for odd, grad, state in ((0, own, states[k]), (1, other, near[k])):
            new = updated(pick(grad, (me >> 1) ^ k, 0), *state)
            owner = me ^ (2 * k + odd)
            weights = lax.dynamic_update_slice(weights, new[0].astype(BF16), (0, owner * cols))
            if k == 0 and odd == 0:
                mine = new
            if odd:
                copies = new if k == 0 else [jnp.where(owner == last, a, b) for a, b in zip(new, copies)]
    return (*mine, weights, *copies)


def shards(grads, master, moment_one, moment_two):
    ng, nf = lax.axis_size("grp"), lax.axis_size("fsdp")
    g_bits, f_bits = ng.bit_length() - 1, nf.bit_length() - 1
    me_f, me_g = lax.axis_index("fsdp"), lax.axis_index("grp")
    core = me_g & 1
    g = grads[0, 0]
    rows, cols = g.shape[0] // nf, g.shape[1] // ng
    cut = cut_up(cols)
    local = rows % 16 == 0 and cols % 128 == 0

    gather = gathered if local else gathered_plain
    (away_out,) = gather(g, [(1, 1)], cut, rows, nf, ng, GLIMIT)
    kept_out, away_own, kept_own = gather(g, [(1, 0), (0, 1), (0, 0)], cut, rows, nf, ng, LIMIT)
    split = lambda t: t.reshape((2,) * (f_bits - 1) + t.shape[2:])
    got_away = [split(swap(t, [1, 1])) for t in away_out]
    sent = [(split(t).astype(F32) + x.astype(F32)).astype(BF16) for t, x in zip(away_own, got_away)]
    got_kept = [split(swap(t, [1, 1])) for t in kept_out]
    kept = [split(t).astype(F32) + x.astype(F32) for t, x in zip(kept_own, got_kept)]

    high = list(range(f_bits - 1, 1, -1))
    labels = [[1] + high, [0] + high]
    orders = [[0, 1, 2], [1, 2, 0]]
    orders = [o + [b for b in range(f_bits) if b not in o] for o in orders]
    for step in range(f_bits):
        masks = [ng << o[step] for o in orders]
        if step == 0:
            held = lax.optimization_barrier(((master, moment_one, moment_two), sent[-1]))[0]
            states = [jnp.stack(held)]
            for b in range(1, g_bits):
                states = states + [swap(s, [1 << b] * 2) for s in states]
        got = [swap(s, masks[::-1] if role(k) else masks) for k, s in enumerate(sent)]

        ts = [k + x.astype(F32) for k, x in zip(kept, got)]
        if step == f_bits - 1:
            break
        want = [o[step + 1] for o in orders]
        a, b = [l.index(w) for l, w in zip(labels, want)]
        bit = [(me_f >> w) & 1 for w in want]

        def choose(t, k, j, away):
            first = (core ^ role(k)) == 0
            if a == b:
                return pick(t, jnp.where(first, bit[0], bit[1]) ^ away, a)
            at = {a: jnp.where(first, bit[0] ^ away, j), b: jnp.where(first, j, bit[1] ^ away)}
            return pick(pick(t, at[max(a, b)], max(a, b)), at[min(a, b)], min(a, b))

        def chosen(t, k, away):
            return choose(t, k, 0, away) if a == b else jnp.stack([choose(t, k, j, away) for j in range(2)])

        sent = [chosen(t, k, 1).astype(BF16) for k, t in enumerate(ts)]
        kept = [chosen(t, k, 0) for k, t in enumerate(ts)]
        rest = [[x for i, x in enumerate(l) if i not in (a, b)] for l in labels]
        labels = rest if a == b else [[labels[0][b]] + rest[0], [labels[1][a]] + rest[1]]

    for b in range(1, g_bits):
        rounded = [t.astype(BF16) for t in ts]
        if b == g_bits - 1:
            states = lax.optimization_barrier((states, rounded[-1]))[0]
            near = [swap(s, [1, 1]) for s in states]

        got = [swap(t, [1 << b] * 2) for t in rounded]
        ts = [t.astype(F32) + x.astype(F32) for t, x in zip(rounded, got)]
    own = [t / (ng * nf) for t in ts]
    other = [swap(t, [1, 1]) for t in own]
    return (finish if local else finish_plain)(own, other, states, near, cols)


def solution(mesh):
    return jax.shard_map(
        shards,
        mesh=mesh,
        in_specs=(P("grp", "fsdp", None, None), P("fsdp", "grp"), P("fsdp", "grp"), P("fsdp", "grp")),
        out_specs=(P("fsdp", "grp"), P("fsdp", "grp"), P("fsdp", "grp"), P("fsdp", None), P("fsdp", "grp"), P("fsdp", "grp"), P("fsdp", "grp")),
        check_vma=False,
    )
```

```python
import functools

import jax
import jax.numpy as jnp
from jax import lax
from jax.experimental import pallas as pl
from jax.experimental.pallas import tpu as pltpu
from jax.sharding import PartitionSpec as P

beta_one = 0.9
beta_two = 0.95
learn_rate = 0.01
decay_rate = 0.1
epsilon = 1e-08
step_count = 100
F32 = jnp.float32
BF16 = jnp.bfloat16
BOTH = ("fsdp", "grp")
SHARES = [1, 1]
ORDERS = [[[0, 1, 2], [1, 2, 0]], [[0, 1, 2], [1, 2, 0]]]
VMEM = pl.BlockSpec(memory_space=pltpu.VMEM)
ANY = pl.BlockSpec(memory_space=pl.ANY)
HBM = pl.BlockSpec(memory_space=pl.ANY)
LIMIT = 4 * 2**20


def swap(x, masks):
    n = lax.axis_size("fsdp") * lax.axis_size("grp")
    return lax.ppermute(x, BOTH, [(i, i ^ masks[i & 1]) for i in range(n)])


def pick(t, index, axis):
    return lax.dynamic_index_in_dim(t, index, axis, keepdims=False)


def updated(gradient, master, moment_one, moment_two):
    new_first = beta_one * moment_one + (1.0 - beta_one) * gradient
    new_second = beta_two * moment_two + (1.0 - beta_two) * gradient * gradient
    first_hat = new_first / (1.0 - beta_one**step_count)
    second_hat = new_second / (1.0 - beta_two**step_count)
    new_master = master - learn_rate * (
        first_hat / (jnp.sqrt(second_hat) + epsilon) + decay_rate * master
    )
    return new_master, new_first, new_second


def cut_up(cols):
    edges = [cols * sum(SHARES[:k]) // sum(SHARES) // 128 * 128 for k in range(len(SHARES))] + [cols]
    return [(a, b - a) for a, b in zip(edges, edges[1:]) if b > a]


def first_block(core, me_f, j, away):
    low, high = me_f & 1, (me_f >> 1) & 1
    return jnp.where(core == 0, low ^ away, j), jnp.where(core == 0, j, high ^ away)


def gathered(g, wanted, cut, rows, nf, ng, limit):
    cols = g.shape[1] // ng
    blocks = g.reshape(nf // 4, 2, 2, rows, g.shape[1])

    def kernel(g_ref, *refs):
        outs, sem = refs[:-1], refs[-1]
        me_f, me_g = lax.axis_index("fsdp"), lax.axis_index("grp")
        moves = []
        for n, (sibling, away) in enumerate(wanted):
            core = (me_g & 1) ^ sibling
            for k, (start, width) in enumerate(cut):
                for j in range(2):
                    low, high = first_block(core, me_f, j, away)
                    for x in range(ng // 2):
                        column = pl.multiple_of((2 * x + core) * cols + start, 128)
                        moves.append(pltpu.make_async_copy(
                            g_ref.at[:, high, low, :, pl.ds(column, width)], outs[n * len(cut) + k].at[j, :, x], sem.at[len(moves)]))
        for m in moves:
            m.start()
        for m in moves:
            m.wait()

    flat = pl.pallas_call(
        kernel,
        out_shape=[jax.ShapeDtypeStruct((2, nf // 4, ng // 2, rows, w), g.dtype) for _ in wanted for _, w in cut],
        in_specs=[HBM],
        out_specs=[VMEM] * (len(wanted) * len(cut)),
        scratch_shapes=[pltpu.SemaphoreType.DMA((ng * len(wanted) * len(cut),))],
        compiler_params=pltpu.CompilerParams(vmem_limit_bytes=limit),
        cost_estimate=pl.CostEstimate(flops=0, bytes_accessed=g.size * len(wanted), transcendentals=0),
    )(blocks)
    return [list(flat[n * len(cut) : (n + 1) * len(cut)]) for n in range(len(wanted))]


def gathered_plain(g, wanted, cut, rows, nf, ng, limit):
    cols = g.shape[1] // ng
    blocks = g.reshape(nf // 4, 2, 2, rows, g.shape[1])
    me_f, me_g = lax.axis_index("fsdp"), lax.axis_index("grp")

    def block(core, k, away, j, x, start, width):
        low, high = first_block(core, me_f, j, away)
        part = lax.dynamic_slice(blocks, (0, high, low, 0, (2 * x + core) * cols + start), (nf // 4, 1, 1, rows, width))
        return part[:, 0, 0]

    return [
        [jnp.stack([jnp.stack([block((me_g & 1) ^ sibling, k, away, j, x, a, w) for x in range(ng // 2)], 1) for j in range(2)]) for k, (a, w) in enumerate(cut)]
        for sibling, away in wanted
    ]


def finish(own, other, states, near, cols):
    parts, rows = len(own), own[0].shape[1]
    ng = 2 * len(states)
    edges = cut_up(cols)

    def kernel(first, *refs):
        refs = list(refs)
        take = lambda n: [refs.pop(0) for _ in range(n)]
        own = take(parts) if first else []
        other = dict(zip(range(parts - 1) if first else [parts - 1], take(parts - 1 if first else 1)))
        states, near = take(ng // 2) if first else [], take(ng // 2)
        if first:
            outs = take(3)
        else:
            take(4)
        weights, copies = take(1)[0], take(3)
        wide, thin, sem = take(3)
        me = lax.axis_index("grp")
        last = lax.rem(me + ng - 1, ng)
        moves = []

        def move(source, target):
            moves.append(pltpu.make_async_copy(source, target, sem.at[len(moves)]))
            moves[-1].start()

        def block(n, part, state, x, edge, keep):
            start, width = edge
            new = updated(part[x], *[state[i, :, start : start + width] for i in range(3)])
            thin[n, :, start : start + width] = new[0].astype(BF16)
            if keep:
                for i in range(3):
                    wide[i, :, start : start + width] = new[i]

        for k in range(len(states)):
            for part, edge in zip(own, edges):
                block(2 * k, part, states[k], (me >> 1) ^ k, edge, k == 0)
            if k == 0:
                for i in range(3):
                    move(wide.at[i], outs[i])
            move(thin.at[2 * k], weights.at[:, pl.ds(pl.multiple_of((me ^ (2 * k)) * cols, 128), cols)])
        for index, part in other.items():
            start, width = edges[index]
            here = pl.ds(start, width)
            for k in range(ng // 2):
                @pl.when((me ^ last) >> 1 == k)
                def _():
                    new = updated(part[last >> 1], *[near[k][i, :, start : start + width] for i in range(3)])
                    for i in range(3):
                        wide[3 + i, :, start : start + width] = new[i]
            for i in range(3):
                move(wide.at[3 + i, :, here], copies[i].at[:, here])
            for k in range(ng // 2):
                block(2 * k + 1, part, near[k], (me >> 1) ^ k, edges[index], False)
                column = pl.multiple_of((me ^ (2 * k + 1)) * cols + start, 128)
                move(thin.at[2 * k + 1, :, here], weights.at[:, pl.ds(column, width)])
        for m in moves:
            m.wait()

    shape = jax.ShapeDtypeStruct((rows, cols), F32)
    shapes = [jax.ShapeDtypeStruct((rows, cols * ng), BF16)] + [shape] * 3
    scratch = [pltpu.VMEM((6, rows, cols), F32), pltpu.VMEM((ng, rows, cols), BF16)]
    early = pl.pallas_call(
        functools.partial(kernel, True),
        out_shape=[shape] * 3 + shapes,
        in_specs=[VMEM] * (2 * parts - 1 + ng),
        out_specs=[ANY] * 7,
        scratch_shapes=scratch + [pltpu.SemaphoreType.DMA((3 + ng // 2 + (3 + ng // 2) * (parts - 1),))],
        cost_estimate=pl.CostEstimate(flops=40 * rows * cols * ng, bytes_accessed=12 * rows * cols * ng, transcendentals=0),
        compiler_params=pltpu.CompilerParams(vmem_limit_bytes=LIMIT),
    )(*own, *other[:-1], *states, *near)
    late = pl.pallas_call(
        functools.partial(kernel, False),
        out_shape=shapes,
        in_specs=[VMEM] * (1 + ng // 2) + [ANY] * 4,
        out_specs=[ANY] * 4,
        scratch_shapes=scratch + [pltpu.SemaphoreType.DMA((3 + ng // 2,))],
        input_output_aliases={1 + ng // 2 + i: i for i in range(4)},
        compiler_params=pltpu.CompilerParams(vmem_limit_bytes=LIMIT),
    )(other[-1], *near, *early[3:])
    return (*early[:3], *late)


def finish_plain(own, other, states, near, cols):
    me = lax.axis_index("grp")
    own, other = jnp.concatenate(own, -1), jnp.concatenate(other, -1)
    ng = 2 * len(states)
    weights = jnp.zeros((own.shape[1], cols * ng), BF16)
    last = (me + ng - 1) % ng
    for k in range(ng // 2):
        for odd, grad, state in ((0, own, states[k]), (1, other, near[k])):
            new = updated(pick(grad, (me >> 1) ^ k, 0), *state)
            owner = me ^ (2 * k + odd)
            weights = lax.dynamic_update_slice(weights, new[0].astype(BF16), (0, owner * cols))
            if k == 0 and odd == 0:
                mine = new
            if odd:
                copies = new if k == 0 else [jnp.where(owner == last, a, b) for a, b in zip(new, copies)]
    return (*mine, weights, *copies)


def onward(t, core, me_f, labels, want):
    a, b = [names.index(w) for names, w in zip(labels, want)]
    bit = [(me_f >> w) & 1 for w in want]

    def choose(j, away):
        if a == b:
            return pick(t, jnp.where(core == 0, bit[0], bit[1]) ^ away, a)
        at = {a: jnp.where(core == 0, bit[0] ^ away, j), b: jnp.where(core == 0, j, bit[1] ^ away)}
        return pick(pick(t, at[max(a, b)], max(a, b)), at[min(a, b)], min(a, b))

    def chosen(away):
        return choose(0, away) if a == b else jnp.stack([choose(j, away) for j in range(2)])

    rest = [[name for i, name in enumerate(names) if i not in (a, b)] for names in labels]
    left = rest if a == b else [[labels[0][b]] + rest[0], [labels[1][a]] + rest[1]]
    return chosen(1).astype(BF16), chosen(0), left


def shards(grads, master, moment_one, moment_two):
    ng, nf = lax.axis_size("grp"), lax.axis_size("fsdp")
    g_bits, f_bits = ng.bit_length() - 1, nf.bit_length() - 1
    me_f, me_g = lax.axis_index("fsdp"), lax.axis_index("grp")
    core = me_g & 1
    g = grads[0, 0]
    rows, cols = g.shape[0] // nf, g.shape[1] // ng
    cut = cut_up(cols)
    local = rows % 16 == 0 and cols % 128 == 0

    gather = gathered if local else gathered_plain
    away_out, away_own = [], []
    source = g
    for edge in cut:
        (out,), (mine,) = gather(source, [(1, 1), (0, 1)], [edge], rows, nf, ng, LIMIT)
        source = lax.optimization_barrier((g, out))[0]
        away_out.append(out)
        away_own.append(mine)
    split = lambda t: t.reshape((2,) * (f_bits - 1) + t.shape[2:])
    got_away = [split(swap(t, [1, 1])) for t in away_out]
    sent = [(split(t).astype(F32) + x.astype(F32)).astype(BF16) for t, x in zip(away_own, got_away)]
    later = lax.optimization_barrier((g, sent[-1]))[0]
    kept_out, kept_own = gather(later, [(1, 0), (0, 0)], cut, rows, nf, ng, LIMIT)
    got_kept = [split(swap(t, [1, 1])) for t in kept_out]
    kept = [split(t).astype(F32) + x.astype(F32) for t, x in zip(kept_own, got_kept)]

    high = list(range(f_bits - 1, 1, -1))
    labels = [[[1] + high, [0] + high] for _ in cut]
    orders = [[o + [b for b in range(f_bits) if b not in o] for o in ORDERS[k % 2]] for k in range(len(cut))]
    for step in range(f_bits):
        masks = [[ng << o[step] for o in pair] for pair in orders]
        if step == 0:
            held = lax.optimization_barrier(((master, moment_one, moment_two), sent[-1]))[0]
            states = [jnp.stack(held)]
            for b in range(1, g_bits):
                states = states + [swap(s, [1 << b] * 2) for s in states]
        got = [swap(s, m) for s, m in zip(sent, masks)]

        ts = [k + x.astype(F32) for k, x in zip(kept, got)]
        if step == f_bits - 1:
            break
        moved = [onward(t, core, me_f, pair, [o[step + 1] for o in order]) for t, pair, order in zip(ts, labels, orders)]
        sent, kept, labels = [list(m) for m in zip(*moved)]

    for b in range(1, g_bits):
        rounded = [t.astype(BF16) for t in ts]
        if b == g_bits - 1:
            states = lax.optimization_barrier((states, rounded[-1]))[0]
            near = [swap(s, [1, 1]) for s in states]

        got = [swap(t, [1 << b] * 2) for t in rounded]
        ts = [t.astype(F32) + x.astype(F32) for t, x in zip(rounded, got)]
    own = [t / (ng * nf) for t in ts]
    other = [swap(t, [1, 1]) for t in own]
    return (finish if local else finish_plain)(own, other, states, near, cols)


def solution(mesh):
    return jax.shard_map(
        shards,
        mesh=mesh,
        in_specs=(P("grp", "fsdp", None, None), P("fsdp", "grp"), P("fsdp", "grp"), P("fsdp", "grp")),
        out_specs=(P("fsdp", "grp"), P("fsdp", "grp"), P("fsdp", "grp"), P("fsdp", None), P("fsdp", "grp"), P("fsdp", "grp"), P("fsdp", "grp")),
        check_vma=False,
    )
```

```python
import functools

import jax
import jax.numpy as jnp
from jax import lax
from jax.experimental import pallas as pl
from jax.experimental.pallas import tpu as pltpu
from jax.sharding import PartitionSpec as P

beta_one = 0.9
beta_two = 0.95
learn_rate = 0.01
decay_rate = 0.1
epsilon = 1e-08
step_count = 100
F32 = jnp.float32
BF16 = jnp.bfloat16
BOTH = ("fsdp", "grp")
SHARES = [1, 1]
ORDERS = [[1, 0], [0, 1]]
VMEM = pl.BlockSpec(memory_space=pltpu.VMEM)
ANY = pl.BlockSpec(memory_space=pl.ANY)
LIMIT = 4 * 2**20


def swap(x, masks):
    n = lax.axis_size("fsdp") * lax.axis_size("grp")
    return lax.ppermute(x, BOTH, [(i, i ^ masks[i & 1]) for i in range(n)])


def pick(t, index, axis):
    return lax.dynamic_index_in_dim(t, index, axis, keepdims=False)


def updated(gradient, master, moment_one, moment_two):
    new_first = beta_one * moment_one + (1.0 - beta_one) * gradient
    new_second = beta_two * moment_two + (1.0 - beta_two) * gradient * gradient
    first_hat = new_first / (1.0 - beta_one**step_count)
    second_hat = new_second / (1.0 - beta_two**step_count)
    new_master = master - learn_rate * (
        first_hat / (jnp.sqrt(second_hat) + epsilon) + decay_rate * master
    )
    return new_master, new_first, new_second


def cut_up(cols):
    edges = [cols * sum(SHARES[:k]) // sum(SHARES) // 128 * 128 for k in range(len(SHARES))] + [cols]
    return [(a, b - a) for a, b in zip(edges, edges[1:]) if b > a]


def first_block(core, me_f, j, away):
    low, high = me_f & 1, (me_f >> 1) & 1
    return jnp.where(core == 0, j, low ^ away), jnp.where(core == 0, high ^ away, j)


def gathered(g, wanted, cut, rows, nf, ng):
    cols = g.shape[1] // ng
    blocks = g.reshape(nf // 4, 2, 2, rows, g.shape[1])

    def kernel(g_ref, *refs):
        outs, sem = refs[:-1], refs[-1]
        me_f, me_g = lax.axis_index("fsdp"), lax.axis_index("grp")
        moves = []
        for n, (sibling, away) in enumerate(wanted):
            core = (me_g & 1) ^ sibling
            for k, (start, width) in enumerate(cut):
                for j in range(2):
                    low, high = first_block(core, me_f, j, away)
                    for x in range(ng // 2):
                        column = pl.multiple_of((2 * x + core) * cols + start, 128)
                        moves.append(pltpu.make_async_copy(
                            g_ref.at[:, high, low, :, pl.ds(column, width)], outs[n * len(cut) + k].at[j, :, x], sem.at[len(moves)]))
        for m in moves:
            m.start()
        for m in moves:
            m.wait()

    flat = pl.pallas_call(
        kernel,
        out_shape=[jax.ShapeDtypeStruct((2, nf // 4, ng // 2, rows, w), g.dtype) for _ in wanted for _, w in cut],
        in_specs=[ANY],
        out_specs=[VMEM] * (len(wanted) * len(cut)),
        scratch_shapes=[pltpu.SemaphoreType.DMA((ng * len(wanted) * len(cut),))],
        compiler_params=pltpu.CompilerParams(vmem_limit_bytes=LIMIT),
        cost_estimate=pl.CostEstimate(flops=0, bytes_accessed=g.size * len(wanted), transcendentals=0),
    )(blocks)
    return [list(flat[n * len(cut) : (n + 1) * len(cut)]) for n in range(len(wanted))]


def gathered_plain(g, wanted, cut, rows, nf, ng):
    cols = g.shape[1] // ng
    blocks = g.reshape(nf // 4, 2, 2, rows, g.shape[1])
    me_f, me_g = lax.axis_index("fsdp"), lax.axis_index("grp")

    def block(core, away, j, x, start, width):
        low, high = first_block(core, me_f, j, away)
        part = lax.dynamic_slice(blocks, (0, high, low, 0, (2 * x + core) * cols + start), (nf // 4, 1, 1, rows, width))
        return part[:, 0, 0]

    return [
        [jnp.stack([jnp.stack([block((me_g & 1) ^ sibling, away, j, x, a, w) for x in range(ng // 2)], 1) for j in range(2)]) for a, w in cut]
        for sibling, away in wanted
    ]


def finish(own, other, states, near, cols):
    parts, rows = len(own), own[0].shape[1]
    ng = 2 * len(states)
    edges = cut_up(cols)

    def kernel(first, *refs):
        refs = list(refs)
        take = lambda n: [refs.pop(0) for _ in range(n)]
        own = take(parts) if first else []
        other = dict(zip(range(parts - 1) if first else [parts - 1], take(parts - 1 if first else 1)))
        states, near = take(ng // 2) if first else [], take(ng // 2)
        if first:
            outs = take(3)
        else:
            take(4)
        weights, copies = take(1)[0], take(3)
        wide, thin, sem = take(3)
        me = lax.axis_index("grp")
        last = lax.rem(me + ng - 1, ng)
        moves = []

        def move(source, target):
            moves.append(pltpu.make_async_copy(source, target, sem.at[len(moves)]))
            moves[-1].start()

        def block(n, part, state, x, edge, keep):
            start, width = edge
            new = updated(part[x], *[state[i, :, start : start + width] for i in range(3)])
            thin[n, :, start : start + width] = new[0].astype(BF16)
            if keep:
                for i in range(3):
                    wide[i, :, start : start + width] = new[i]

        for k in range(len(states)):
            for part, edge in zip(own, edges):
                block(2 * k, part, states[k], (me >> 1) ^ k, edge, k == 0)
            if k == 0:
                for i in range(3):
                    move(wide.at[i], outs[i])
            move(thin.at[2 * k], weights.at[:, pl.ds(pl.multiple_of((me ^ (2 * k)) * cols, 128), cols)])
        for index, part in other.items():
            start, width = edges[index]
            here = pl.ds(start, width)
            for k in range(ng // 2):
                @pl.when((me ^ last) >> 1 == k)
                def _():
                    new = updated(part[last >> 1], *[near[k][i, :, start : start + width] for i in range(3)])
                    for i in range(3):
                        wide[3 + i, :, start : start + width] = new[i]
            for i in range(3):
                move(wide.at[3 + i, :, here], copies[i].at[:, here])
            for k in range(ng // 2):
                block(2 * k + 1, part, near[k], (me >> 1) ^ k, edges[index], False)
                column = pl.multiple_of((me ^ (2 * k + 1)) * cols + start, 128)
                move(thin.at[2 * k + 1, :, here], weights.at[:, pl.ds(column, width)])
        for m in moves:
            m.wait()

    shape = jax.ShapeDtypeStruct((rows, cols), F32)
    shapes = [jax.ShapeDtypeStruct((rows, cols * ng), BF16)] + [shape] * 3
    scratch = [pltpu.VMEM((6, rows, cols), F32), pltpu.VMEM((ng, rows, cols), BF16)]
    early = pl.pallas_call(
        functools.partial(kernel, True),
        out_shape=[shape] * 3 + shapes,
        in_specs=[VMEM] * (2 * parts - 1 + ng),
        out_specs=[ANY] * 7,
        scratch_shapes=scratch + [pltpu.SemaphoreType.DMA((3 + ng // 2 + (3 + ng // 2) * (parts - 1),))],
        cost_estimate=pl.CostEstimate(flops=40 * rows * cols * ng, bytes_accessed=12 * rows * cols * ng, transcendentals=0),
        compiler_params=pltpu.CompilerParams(vmem_limit_bytes=LIMIT),
    )(*own, *other[:-1], *states, *near)
    late = pl.pallas_call(
        functools.partial(kernel, False),
        out_shape=shapes,
        in_specs=[VMEM] * (1 + ng // 2) + [ANY] * 4,
        out_specs=[ANY] * 4,
        scratch_shapes=scratch + [pltpu.SemaphoreType.DMA((3 + ng // 2,))],
        input_output_aliases={1 + ng // 2 + i: i for i in range(4)},
        compiler_params=pltpu.CompilerParams(vmem_limit_bytes=LIMIT),
    )(other[-1], *near, *early[3:])
    return (*early[:3], *late)


def finish_plain(own, other, states, near, cols):
    me = lax.axis_index("grp")
    own, other = jnp.concatenate(own, -1), jnp.concatenate(other, -1)
    ng = 2 * len(states)
    gradient = jnp.stack([pick((own, other)[r & 1], (me >> 1) ^ (r >> 1), 0) for r in range(ng)])
    state = jnp.stack([(states, near)[r & 1][r >> 1] for r in range(ng)])
    new = updated(gradient, state[:, 0], state[:, 1], state[:, 2])
    blocks = new[0].astype(BF16)
    weights = jnp.zeros((own.shape[1], cols * ng), BF16)
    for r in range(ng):
        weights = lax.dynamic_update_slice(weights, blocks[r], (0, (me ^ r) * cols))
    last = (me + ng - 1) % ng
    return (*[n[0] for n in new], weights, *[pick(n, me ^ last, 0) for n in new])


def onward(t, core, me_f, labels, want):
    a, b = [names.index(w) for names, w in zip(labels, want)]
    bit = [(me_f >> w) & 1 for w in want]

    def choose(j, away):
        if a == b:
            return pick(t, jnp.where(core == 0, bit[0], bit[1]) ^ away, a)
        at = {a: jnp.where(core == 0, bit[0] ^ away, j), b: jnp.where(core == 0, j, bit[1] ^ away)}
        return pick(pick(t, at[max(a, b)], max(a, b)), at[min(a, b)], min(a, b))

    def chosen(away):
        return choose(0, away) if a == b else jnp.stack([choose(j, away) for j in range(2)])

    rest = [[name for i, name in enumerate(names) if i not in (a, b)] for names in labels]
    left = rest if a == b else [[labels[0][b]] + rest[0], [labels[1][a]] + rest[1]]
    return chosen(1).astype(BF16), chosen(0), left


def shards(grads, master, moment_one, moment_two):
    ng, nf = lax.axis_size("grp"), lax.axis_size("fsdp")
    g_bits, f_bits = ng.bit_length() - 1, nf.bit_length() - 1
    me_f, me_g = lax.axis_index("fsdp"), lax.axis_index("grp")
    core = me_g & 1
    g = grads[0, 0]
    rows, cols = g.shape[0] // nf, g.shape[1] // ng
    cut = cut_up(cols)
    local = rows % 16 == 0 and cols % 128 == 0

    gather = gathered if local else gathered_plain
    away_out, away_own = [], []
    for edge in cut:
        (out,), (mine,) = gather(g, [(1, 1), (0, 1)], [edge], rows, nf, ng)
        away_out.append(out)
        away_own.append(mine)
    split = lambda t: t.reshape((2,) * (f_bits - 1) + t.shape[2:])
    got_away = [split(swap(t, [1, 1])) for t in away_out]
    sent = [(split(t).astype(F32) + x.astype(F32)).astype(BF16) for t, x in zip(away_own, got_away)]
    later = lax.optimization_barrier((g, sent[-1]))[0]
    kept_out, kept_own = gather(later, [(1, 0), (0, 0)], cut, rows, nf, ng)
    got_kept = [split(swap(t, [1, 1])) for t in kept_out]
    kept = [split(t).astype(F32) + x.astype(F32) for t, x in zip(kept_own, got_kept)]

    high = list(range(f_bits - 1, 1, -1))
    labels = [[[0] + high, [1] + high] for _ in cut]
    orders = [o + list(range(len(o), f_bits)) for o in ORDERS]
    for step in range(f_bits):
        masks = [ng << o[step] for o in orders]
        if step == 0:
            held = lax.optimization_barrier(((master, moment_one, moment_two), sent[-1]))[0]
            states = [jnp.stack(held)]
            for b in range(1, g_bits):
                states = states + [swap(s, [1 << b] * 2) for s in states]
        got = [swap(s, masks) for s in sent]
        ts = [k + x.astype(F32) for k, x in zip(kept, got)]
        if step == f_bits - 1:
            break
        want = [o[step + 1] for o in orders]
        moved = [onward(t, core, me_f, names, want) for t, names in zip(ts, labels)]
        sent, kept, labels = [list(m) for m in zip(*moved)]

    for b in range(1, g_bits):
        rounded = [t.astype(BF16) for t in ts]
        if b == g_bits - 1:
            states = lax.optimization_barrier((states, rounded[-1]))[0]
            near = [swap(s, [1, 1]) for s in states]
        got = [swap(t, [1 << b] * 2) for t in rounded]
        ts = [t.astype(F32) + x.astype(F32) for t, x in zip(rounded, got)]
    own = [t / (ng * nf) for t in ts]
    other = [swap(t, [1, 1]) for t in own]
    return (finish if local else finish_plain)(own, other, states, near, cols)


def solution(mesh):
    return jax.shard_map(
        shards,
        mesh=mesh,
        in_specs=(P("grp", "fsdp", None, None), P("fsdp", "grp"), P("fsdp", "grp"), P("fsdp", "grp")),
        out_specs=(P("fsdp", "grp"), P("fsdp", "grp"), P("fsdp", "grp"), P("fsdp", None), P("fsdp", "grp"), P("fsdp", "grp"), P("fsdp", "grp")),
        check_vma=False,
    )
```

```python
import functools

import jax
import jax.numpy as jnp
from jax import lax
from jax.experimental import pallas as pl
from jax.experimental.pallas import tpu as pltpu
from jax.sharding import PartitionSpec as P

beta_one = 0.9
beta_two = 0.95
learn_rate = 0.01
decay_rate = 0.1
epsilon = 1e-08
step_count = 100
F32 = jnp.float32
BF16 = jnp.bfloat16
BOTH = ("fsdp", "grp")
SHARES = [1, 1]
ORDERS = [[1, 0], [0, 1]]
VMEM = pl.BlockSpec(memory_space=pltpu.VMEM)
ANY = pl.BlockSpec(memory_space=pl.ANY)
LIMIT = 4 * 2**20


def swap(x, masks):
    n = lax.axis_size("fsdp") * lax.axis_size("grp")
    return lax.ppermute(x, BOTH, [(i, i ^ masks[i & 1]) for i in range(n)])


def pick(t, index, axis):
    return lax.dynamic_index_in_dim(t, index, axis, keepdims=False)


def updated(gradient, master, moment_one, moment_two):
    new_first = beta_one * moment_one + (1.0 - beta_one) * gradient
    new_second = beta_two * moment_two + (1.0 - beta_two) * gradient * gradient
    first_hat = new_first / (1.0 - beta_one**step_count)
    second_hat = new_second / (1.0 - beta_two**step_count)
    new_master = master - learn_rate * (
        first_hat / (jnp.sqrt(second_hat) + epsilon) + decay_rate * master
    )
    return new_master, new_first, new_second


def cut_up(cols):
    edges = [cols * sum(SHARES[:k]) // sum(SHARES) // 128 * 128 for k in range(len(SHARES))] + [cols]
    return [(a, b - a) for a, b in zip(edges, edges[1:]) if b > a]


def first_block(core, me_f, j, away):
    low, high = me_f & 1, (me_f >> 1) & 1
    return jnp.where(core == 0, j, low ^ away), jnp.where(core == 0, high ^ away, j)


def gathered(g, wanted, cut, rows, nf, ng):
    cols = g.shape[1] // ng
    blocks = g.reshape(nf // 4, 2, 2, rows, g.shape[1])

    def kernel(g_ref, *refs):
        outs, sem = refs[:-1], refs[-1]
        me_f, me_g = lax.axis_index("fsdp"), lax.axis_index("grp")
        moves = []
        for n, (sibling, away) in enumerate(wanted):
            core = (me_g & 1) ^ sibling
            for k, (start, width) in enumerate(cut):
                for j in range(2):
                    low, high = first_block(core, me_f, j, away)
                    for x in range(ng // 2):
                        column = pl.multiple_of((2 * x + core) * cols + start, 128)
                        moves.append(pltpu.make_async_copy(
                            g_ref.at[:, high, low, :, pl.ds(column, width)], outs[n * len(cut) + k].at[j, :, x], sem.at[len(moves)]))
        for m in moves:
            m.start()
        for m in moves:
            m.wait()

    flat = pl.pallas_call(
        kernel,
        out_shape=[jax.ShapeDtypeStruct((2, nf // 4, ng // 2, rows, w), g.dtype) for _ in wanted for _, w in cut],
        in_specs=[ANY],
        out_specs=[VMEM] * (len(wanted) * len(cut)),
        scratch_shapes=[pltpu.SemaphoreType.DMA((ng * len(wanted) * len(cut),))],
        compiler_params=pltpu.CompilerParams(vmem_limit_bytes=LIMIT),
        cost_estimate=pl.CostEstimate(flops=0, bytes_accessed=g.size * len(wanted), transcendentals=0),
    )(blocks)
    return [list(flat[n * len(cut) : (n + 1) * len(cut)]) for n in range(len(wanted))]


def gathered_plain(g, wanted, cut, rows, nf, ng):
    cols = g.shape[1] // ng
    blocks = g.reshape(nf // 4, 2, 2, rows, g.shape[1])
    me_f, me_g = lax.axis_index("fsdp"), lax.axis_index("grp")

    def block(core, away, j, x, start, width):
        low, high = first_block(core, me_f, j, away)
        part = lax.dynamic_slice(blocks, (0, high, low, 0, (2 * x + core) * cols + start), (nf // 4, 1, 1, rows, width))
        return part[:, 0, 0]

    return [
        [jnp.stack([jnp.stack([block((me_g & 1) ^ sibling, away, j, x, a, w) for x in range(ng // 2)], 1) for j in range(2)]) for a, w in cut]
        for sibling, away in wanted
    ]


def finish(own, other, states, near, cols, outs):
    rows = [*own.values(), *other.values()][0].shape[1]
    ng = 2 * len(states)
    edges = cut_up(cols)

    def kernel(mine, theirs, first, *refs):
        refs = list(refs)
        take = lambda n: [refs.pop(0) for _ in range(n)]
        own, other = take(len(mine)), take(len(theirs))
        states, near = take(ng // 2 if mine else 0), take(ng // 2 if theirs else 0)
        take(0 if first else 7)
        outs, weights, copies = take(3), take(1)[0], take(3)
        wide, thin, sem = take(3)
        me = lax.axis_index("grp")
        last = lax.rem(me + ng - 1, ng)
        moves = []

        def move(source, target):
            moves.append(pltpu.make_async_copy(source, target, sem.at[len(moves)]))
            moves[-1].start()

        def fresh(part, x, state, start, width):
            return updated(part[x].astype(F32), *[state[i, :, start : start + width] for i in range(3)])

        def weigh(n, new, start, width):
            thin[n, :, start : start + width] = new[0].astype(BF16)
            column = pl.multiple_of((me ^ n) * cols + start, 128)
            move(thin.at[n, :, pl.ds(start, width)], weights.at[:, pl.ds(column, width)])

        for index, part in zip(mine, own):
            start, width = edges[index]
            for k in range(ng // 2):
                new = fresh(part, (me >> 1) ^ k, states[k], start, width)
                if k == 0:
                    for i in range(3):
                        wide[i, :, start : start + width] = new[i]
                        move(wide.at[i, :, pl.ds(start, width)], outs[i].at[:, pl.ds(start, width)])
                weigh(2 * k, new, start, width)
        for index, part in zip(theirs, other):
            start, width = edges[index]
            for k in range(ng // 2):
                @pl.when((me ^ last) >> 1 == k)
                def _():
                    new = fresh(part, last >> 1, near[k], start, width)
                    for i in range(3):
                        wide[3 + i, :, start : start + width] = new[i]
            for i in range(3):
                move(wide.at[3 + i, :, pl.ds(start, width)], copies[i].at[:, pl.ds(start, width)])
            for k in range(ng // 2):
                weigh(2 * k + 1, fresh(part, (me >> 1) ^ k, near[k], start, width), start, width)
        for m in moves:
            m.wait()

    shape = jax.ShapeDtypeStruct((rows, cols), F32)
    shapes = [shape] * 3 + [jax.ShapeDtypeStruct((rows, cols * ng), BF16)] + [shape] * 3
    given = list(own.values()) + list(other.values()) + (states if own else []) + (near if other else [])
    return pl.pallas_call(
        functools.partial(kernel, list(own), list(other), not outs),
        out_shape=shapes,
        in_specs=[VMEM] * len(given) + [ANY] * len(outs),
        out_specs=[ANY] * 7,
        scratch_shapes=[
            pltpu.VMEM((6, rows, cols), F32),
            pltpu.VMEM((ng, rows, cols), BF16),
            pltpu.SemaphoreType.DMA(((3 + ng // 2) * (len(own) + len(other)),)),
        ],
        input_output_aliases={len(given) + i: i for i in range(len(outs))},
        cost_estimate=pl.CostEstimate(flops=40 * rows * cols * ng, bytes_accessed=12 * rows * cols * ng, transcendentals=0),
        compiler_params=pltpu.CompilerParams(vmem_limit_bytes=LIMIT),
    )(*given, *outs)


def finish_plain(own, other, states, near, cols):
    me = lax.axis_index("grp")
    own, other = jnp.concatenate(own, -1), jnp.concatenate(other, -1)
    ng = 2 * len(states)
    gradient = jnp.stack([pick((own, other)[r & 1], (me >> 1) ^ (r >> 1), 0) for r in range(ng)])
    state = jnp.stack([(states, near)[r & 1][r >> 1] for r in range(ng)])
    new = updated(gradient, state[:, 0], state[:, 1], state[:, 2])
    blocks = new[0].astype(BF16)
    weights = jnp.zeros((own.shape[1], cols * ng), BF16)
    for r in range(ng):
        weights = lax.dynamic_update_slice(weights, blocks[r], (0, (me ^ r) * cols))
    last = (me + ng - 1) % ng
    return (*[n[0] for n in new], weights, *[pick(n, me ^ last, 0) for n in new])


def onward(t, core, me_f, labels, want):
    a, b = [names.index(w) for names, w in zip(labels, want)]
    bit = [(me_f >> w) & 1 for w in want]

    def choose(j, away):
        if a == b:
            return pick(t, jnp.where(core == 0, bit[0], bit[1]) ^ away, a)
        at = {a: jnp.where(core == 0, bit[0] ^ away, j), b: jnp.where(core == 0, j, bit[1] ^ away)}
        return pick(pick(t, at[max(a, b)], max(a, b)), at[min(a, b)], min(a, b))

    def chosen(away):
        return choose(0, away) if a == b else jnp.stack([choose(j, away) for j in range(2)])

    rest = [[name for i, name in enumerate(names) if i not in (a, b)] for names in labels]
    left = rest if a == b else [[labels[0][b]] + rest[0], [labels[1][a]] + rest[1]]
    return chosen(1).astype(BF16), chosen(0), left


def shards(grads, master, moment_one, moment_two):
    ng, nf = lax.axis_size("grp"), lax.axis_size("fsdp")
    g_bits, f_bits = ng.bit_length() - 1, nf.bit_length() - 1
    me_f, me_g = lax.axis_index("fsdp"), lax.axis_index("grp")
    core = me_g & 1
    g = grads[0, 0]
    rows, cols = g.shape[0] // nf, g.shape[1] // ng
    cut = cut_up(cols)
    local = rows % 16 == 0 and cols % 128 == 0

    gather = gathered if local else gathered_plain
    away_out, away_own = [], []
    for edge in cut:
        (out,), (mine,) = gather(g, [(1, 1), (0, 1)], [edge], rows, nf, ng)
        away_out.append(out)
        away_own.append(mine)
    scaled = lambda t: t / (ng * nf)
    outs = []
    split = lambda t: t.reshape((2,) * (f_bits - 1) + t.shape[2:])
    got_away = [split(swap(t, [1, 1])) for t in away_out]
    sent = [(split(t).astype(F32) + x.astype(F32)).astype(BF16) for t, x in zip(away_own, got_away)]
    later = lax.optimization_barrier((g, sent[-1]))[0]
    kept_out, kept_own = gather(later, [(1, 0), (0, 0)], cut, rows, nf, ng)
    got_kept = [split(swap(t, [1, 1])) for t in kept_out]
    kept = [split(t).astype(F32) + x.astype(F32) for t, x in zip(kept_own, got_kept)]

    high = list(range(f_bits - 1, 1, -1))
    labels = [[[0] + high, [1] + high] for _ in cut]
    orders = [o + list(range(len(o), f_bits)) for o in ORDERS]
    for step in range(f_bits):
        masks = [ng << o[step] for o in orders]
        if step == 0:
            held = lax.optimization_barrier(((master, moment_one, moment_two), sent[-1]))[0]
            states = [jnp.stack(held)]
            for b in range(1, g_bits):
                states = states + [swap(s, [1 << b] * 2) for s in states]
        got = [swap(s, masks) for s in sent]
        ts = [k + x.astype(F32) for k, x in zip(kept, got)]
        if step == f_bits - 1:
            break
        want = [o[step + 1] for o in orders]
        moved = [onward(t, core, me_f, names, want) for t, names in zip(ts, labels)]
        sent, kept, labels = [list(m) for m in zip(*moved)]

    for b in range(1, g_bits):
        rounded = [t.astype(BF16) for t in ts]
        if b == g_bits - 1:
            states = lax.optimization_barrier((states, rounded[-1]))[0]
            near = [swap(s, [1, 1]) for s in states]
        got = [swap(t, [1 << b] * 2) for t in rounded]
        if local and b == g_bits - 1 and len(cut) > 1:
            head = rounded[0].astype(F32) + got[0].astype(F32)
            outs = finish({0: scaled(head)}, {}, states, None, cols, [])
            rounded[-1] = lax.optimization_barrier((rounded[-1], outs[0]))[0]
        ts = [t.astype(F32) + x.astype(F32) for t, x in zip(rounded, got)]
    own = [scaled(t) for t in ts]
    other = [swap(t, [1, 1]) for t in own]
    if not local:
        return finish_plain(own, other, states, near, cols)
    own, other = dict(enumerate(own)), dict(enumerate(other))
    tail = {max(other): other.pop(max(other))}
    if len(cut) > 1:
        own.pop(0)
    outs = finish(own, other, states, near, cols, outs)
    return tuple(finish({}, tail, states, near, cols, outs))


def solution(mesh):
    return jax.shard_map(
        shards,
        mesh=mesh,
        in_specs=(P("grp", "fsdp", None, None), P("fsdp", "grp"), P("fsdp", "grp"), P("fsdp", "grp")),
        out_specs=(P("fsdp", "grp"), P("fsdp", "grp"), P("fsdp", "grp"), P("fsdp", None), P("fsdp", "grp"), P("fsdp", "grp"), P("fsdp", "grp")),
        check_vma=False,
    )
```

```python
import functools

import jax
import jax.numpy as jnp
from jax import lax
from jax.experimental import pallas as pl
from jax.experimental.pallas import tpu as pltpu
from jax.sharding import PartitionSpec as P

beta_one = 0.9
beta_two = 0.95
learn_rate = 0.01
decay_rate = 0.1
epsilon = 1e-08
step_count = 100
F32 = jnp.float32
BF16 = jnp.bfloat16
BOTH = ("fsdp", "grp")
SHARES = [1, 1]
ORDERS = [[[1, 0], [0, 2]], [[1, 0], [0, 1]]]
VMEM = pl.BlockSpec(memory_space=pltpu.VMEM)
ANY = pl.BlockSpec(memory_space=pl.ANY)
LIMIT = 4 * 2**20


def swap(x, masks):
    n = lax.axis_size("fsdp") * lax.axis_size("grp")
    return lax.ppermute(x, BOTH, [(i, i ^ masks[i & 1]) for i in range(n)])


def pick(t, index, axis):
    return lax.dynamic_index_in_dim(t, index, axis, keepdims=False)


def updated(gradient, master, moment_one, moment_two):
    new_first = beta_one * moment_one + (1.0 - beta_one) * gradient
    new_second = beta_two * moment_two + (1.0 - beta_two) * gradient * gradient
    first_hat = new_first / (1.0 - beta_one**step_count)
    second_hat = new_second / (1.0 - beta_two**step_count)
    new_master = master - learn_rate * (
        first_hat / (jnp.sqrt(second_hat) + epsilon) + decay_rate * master
    )
    return new_master, new_first, new_second


def cut_up(cols):
    edges = [cols * sum(SHARES[:k]) // sum(SHARES) // 128 * 128 for k in range(len(SHARES))] + [cols]
    return [(a, b - a) for a, b in zip(edges, edges[1:]) if b > a]


def first_block(core, me_f, j, away):
    low, high = me_f & 1, (me_f >> 1) & 1
    return jnp.where(core == 0, j, low ^ away), jnp.where(core == 0, high ^ away, j)


def gathered(g, wanted, cut, rows, nf, ng):
    cols = g.shape[1] // ng
    blocks = g.reshape(nf // 4, 2, 2, rows, g.shape[1])

    def kernel(g_ref, *refs):
        outs, sem = refs[:-1], refs[-1]
        me_f, me_g = lax.axis_index("fsdp"), lax.axis_index("grp")
        moves = []
        for n, (sibling, away) in enumerate(wanted):
            core = (me_g & 1) ^ sibling
            for k, (start, width) in enumerate(cut):
                for j in range(2):
                    low, high = first_block(core, me_f, j, away)
                    for x in range(ng // 2):
                        column = pl.multiple_of((2 * x + core) * cols + start, 128)
                        moves.append(pltpu.make_async_copy(
                            g_ref.at[:, high, low, :, pl.ds(column, width)], outs[n * len(cut) + k].at[j, :, x], sem.at[len(moves)]))
        for m in moves:
            m.start()
        for m in moves:
            m.wait()

    flat = pl.pallas_call(
        kernel,
        out_shape=[jax.ShapeDtypeStruct((2, nf // 4, ng // 2, rows, w), g.dtype) for _ in wanted for _, w in cut],
        in_specs=[ANY],
        out_specs=[VMEM] * (len(wanted) * len(cut)),
        scratch_shapes=[pltpu.SemaphoreType.DMA((ng * len(wanted) * len(cut),))],
        compiler_params=pltpu.CompilerParams(vmem_limit_bytes=LIMIT),
        cost_estimate=pl.CostEstimate(flops=0, bytes_accessed=g.size * len(wanted), transcendentals=0),
    )(blocks)
    return [list(flat[n * len(cut) : (n + 1) * len(cut)]) for n in range(len(wanted))]


def gathered_plain(g, wanted, cut, rows, nf, ng):
    cols = g.shape[1] // ng
    blocks = g.reshape(nf // 4, 2, 2, rows, g.shape[1])
    me_f, me_g = lax.axis_index("fsdp"), lax.axis_index("grp")

    def block(core, away, j, x, start, width):
        low, high = first_block(core, me_f, j, away)
        part = lax.dynamic_slice(blocks, (0, high, low, 0, (2 * x + core) * cols + start), (nf // 4, 1, 1, rows, width))
        return part[:, 0, 0]

    return [
        [jnp.stack([jnp.stack([block((me_g & 1) ^ sibling, away, j, x, a, w) for x in range(ng // 2)], 1) for j in range(2)]) for a, w in cut]
        for sibling, away in wanted
    ]


def finish(own, other, states, near, cols):
    parts, rows = len(own), own[0].shape[1]
    ng = 2 * len(states)
    edges = cut_up(cols)

    def kernel(first, *refs):
        refs = list(refs)
        take = lambda n: [refs.pop(0) for _ in range(n)]
        own = take(parts) if first else []
        other = dict(zip(range(parts - 1) if first else [parts - 1], take(parts - 1 if first else 1)))
        states, near = take(ng // 2) if first else [], take(ng // 2)
        if first:
            outs = take(3)
        else:
            take(4)
        weights, copies = take(1)[0], take(3)
        wide, thin, sem = take(3)
        me = lax.axis_index("grp")
        last = lax.rem(me + ng - 1, ng)
        moves = []

        def move(source, target):
            moves.append(pltpu.make_async_copy(source, target, sem.at[len(moves)]))
            moves[-1].start()

        def block(n, part, state, x, edge, keep):
            start, width = edge
            new = updated(part[x], *[state[i, :, start : start + width] for i in range(3)])
            thin[n, :, start : start + width] = new[0].astype(BF16)
            if keep:
                for i in range(3):
                    wide[i, :, start : start + width] = new[i]

        for k in range(len(states)):
            for part, edge in zip(own, edges):
                block(2 * k, part, states[k], (me >> 1) ^ k, edge, k == 0)
            if k == 0:
                for i in range(3):
                    move(wide.at[i], outs[i])
            move(thin.at[2 * k], weights.at[:, pl.ds(pl.multiple_of((me ^ (2 * k)) * cols, 128), cols)])
        for index, part in other.items():
            start, width = edges[index]
            here = pl.ds(start, width)
            for k in range(ng // 2):
                @pl.when((me ^ last) >> 1 == k)
                def _():
                    new = updated(part[last >> 1], *[near[k][i, :, start : start + width] for i in range(3)])
                    for i in range(3):
                        wide[3 + i, :, start : start + width] = new[i]
            for i in range(3):
                move(wide.at[3 + i, :, here], copies[i].at[:, here])
            for k in range(ng // 2):
                block(2 * k + 1, part, near[k], (me >> 1) ^ k, edges[index], False)
                column = pl.multiple_of((me ^ (2 * k + 1)) * cols + start, 128)
                move(thin.at[2 * k + 1, :, here], weights.at[:, pl.ds(column, width)])
        for m in moves:
            m.wait()

    shape = jax.ShapeDtypeStruct((rows, cols), F32)
    shapes = [jax.ShapeDtypeStruct((rows, cols * ng), BF16)] + [shape] * 3
    scratch = [pltpu.VMEM((6, rows, cols), F32), pltpu.VMEM((ng, rows, cols), BF16)]
    early = pl.pallas_call(
        functools.partial(kernel, True),
        out_shape=[shape] * 3 + shapes,
        in_specs=[VMEM] * (2 * parts - 1 + ng),
        out_specs=[ANY] * 7,
        scratch_shapes=scratch + [pltpu.SemaphoreType.DMA((3 + ng // 2 + (3 + ng // 2) * (parts - 1),))],
        cost_estimate=pl.CostEstimate(flops=40 * rows * cols * ng, bytes_accessed=12 * rows * cols * ng, transcendentals=0),
        compiler_params=pltpu.CompilerParams(vmem_limit_bytes=LIMIT),
    )(*own, *other[:-1], *states, *near)
    late = pl.pallas_call(
        functools.partial(kernel, False),
        out_shape=shapes,
        in_specs=[VMEM] * (1 + ng // 2) + [ANY] * 4,
        out_specs=[ANY] * 4,
        scratch_shapes=scratch + [pltpu.SemaphoreType.DMA((3 + ng // 2,))],
        input_output_aliases={1 + ng // 2 + i: i for i in range(4)},
        compiler_params=pltpu.CompilerParams(vmem_limit_bytes=LIMIT),
    )(other[-1], *near, *early[3:])
    return (*early[:3], *late)


def finish_plain(own, other, states, near, cols):
    me = lax.axis_index("grp")
    own, other = jnp.concatenate(own, -1), jnp.concatenate(other, -1)
    ng = 2 * len(states)
    gradient = jnp.stack([pick((own, other)[r & 1], (me >> 1) ^ (r >> 1), 0) for r in range(ng)])
    state = jnp.stack([(states, near)[r & 1][r >> 1] for r in range(ng)])
    new = updated(gradient, state[:, 0], state[:, 1], state[:, 2])
    blocks = new[0].astype(BF16)
    weights = jnp.zeros((own.shape[1], cols * ng), BF16)
    for r in range(ng):
        weights = lax.dynamic_update_slice(weights, blocks[r], (0, (me ^ r) * cols))
    last = (me + ng - 1) % ng
    return (*[n[0] for n in new], weights, *[pick(n, me ^ last, 0) for n in new])


def onward(t, core, me_f, labels, want):
    a, b = [names.index(w) for names, w in zip(labels, want)]
    bit = [(me_f >> w) & 1 for w in want]

    def choose(j, away):
        if a == b:
            return pick(t, jnp.where(core == 0, bit[0], bit[1]) ^ away, a)
        at = {a: jnp.where(core == 0, bit[0] ^ away, j), b: jnp.where(core == 0, j, bit[1] ^ away)}
        return pick(pick(t, at[max(a, b)], max(a, b)), at[min(a, b)], min(a, b))

    def chosen(away):
        return choose(0, away) if a == b else jnp.stack([choose(j, away) for j in range(2)])

    rest = [[name for i, name in enumerate(names) if i not in (a, b)] for names in labels]
    left = rest if a == b else [[labels[0][b]] + rest[0], [labels[1][a]] + rest[1]]
    return chosen(1).astype(BF16), chosen(0), left


def shards(grads, master, moment_one, moment_two):
    ng, nf = lax.axis_size("grp"), lax.axis_size("fsdp")
    g_bits, f_bits = ng.bit_length() - 1, nf.bit_length() - 1
    me_f, me_g = lax.axis_index("fsdp"), lax.axis_index("grp")
    core = me_g & 1
    g = grads[0, 0]
    rows, cols = g.shape[0] // nf, g.shape[1] // ng
    cut = cut_up(cols)
    local = rows % 16 == 0 and cols % 128 == 0

    gather = gathered if local else gathered_plain
    away_out, away_own = [], []
    for edge in cut:
        (out,), (mine,) = gather(g, [(1, 1), (0, 1)], [edge], rows, nf, ng)
        away_out.append(out)
        away_own.append(mine)
    split = lambda t: t.reshape((2,) * (f_bits - 1) + t.shape[2:])
    got_away = [split(swap(t, [1, 1])) for t in away_out]
    sent = [(split(t).astype(F32) + x.astype(F32)).astype(BF16) for t, x in zip(away_own, got_away)]
    later = lax.optimization_barrier((g, sent[-1]))[0]
    kept_out, kept_own = gather(later, [(1, 0), (0, 0)], cut, rows, nf, ng)
    got_kept = [split(swap(t, [1, 1])) for t in kept_out]
    kept = [split(t).astype(F32) + x.astype(F32) for t, x in zip(kept_own, got_kept)]

    high = list(range(f_bits - 1, 1, -1))
    labels = [[[0] + high, [1] + high] for _ in cut]
    orders = [[o + [b for b in range(f_bits) if b not in o] for o in ORDERS[k % 2]] for k in range(len(cut))]
    for step in range(f_bits):
        masks = [[ng << o[step] for o in pair] for pair in orders]
        if step == 0:
            held = lax.optimization_barrier(((master, moment_one, moment_two), sent[-1]))[0]
            states = [jnp.stack(held)]
            for b in range(1, g_bits):
                states = states + [swap(s, [1 << b] * 2) for s in states]
        got = [swap(s, m) for s, m in zip(sent, masks)]
        ts = [k + x.astype(F32) for k, x in zip(kept, got)]
        if step == f_bits - 1:
            break
        moved = [onward(t, core, me_f, names, [o[step + 1] for o in pair]) for t, names, pair in zip(ts, labels, orders)]
        sent, kept, labels = [list(m) for m in zip(*moved)]

    for b in range(1, g_bits):
        rounded = [t.astype(BF16) for t in ts]
        if b == g_bits - 1:
            states = lax.optimization_barrier((states, rounded[-1]))[0]
            near = [swap(s, [1, 1]) for s in states]
        got = [swap(t, [1 << b] * 2) for t in rounded]
        ts = [t.astype(F32) + x.astype(F32) for t, x in zip(rounded, got)]
    own = [t / (ng * nf) for t in ts]
    other = [swap(t, [1, 1]) for t in own]
    return (finish if local else finish_plain)(own, other, states, near, cols)


def solution(mesh):
    return jax.shard_map(
        shards,
        mesh=mesh,
        in_specs=(P("grp", "fsdp", None, None), P("fsdp", "grp"), P("fsdp", "grp"), P("fsdp", "grp")),
        out_specs=(P("fsdp", "grp"), P("fsdp", "grp"), P("fsdp", "grp"), P("fsdp", None), P("fsdp", "grp"), P("fsdp", "grp"), P("fsdp", "grp")),
        check_vma=False,
    )
```

```python
import functools

import jax
import jax.numpy as jnp
from jax import lax
from jax.experimental import pallas as pl
from jax.experimental.pallas import tpu as pltpu
from jax.sharding import PartitionSpec as P

beta_one = 0.9
beta_two = 0.95
learn_rate = 0.01
decay_rate = 0.1
epsilon = 1e-08
step_count = 100
F32 = jnp.float32
BF16 = jnp.bfloat16
BOTH = ("fsdp", "grp")
SHARES = [1, 1]
ORDERS = [[1, 0], [0, 1]]
VMEM = pl.BlockSpec(memory_space=pltpu.VMEM)
ANY = pl.BlockSpec(memory_space=pl.ANY)
LIMIT = 4 * 2**20


def swap(x, masks):
    n = lax.axis_size("fsdp") * lax.axis_size("grp")
    return lax.ppermute(x, BOTH, [(i, i ^ masks[i & 1]) for i in range(n)])


def pick(t, index, axis):
    return lax.dynamic_index_in_dim(t, index, axis, keepdims=False)


def updated(gradient, master, moment_one, moment_two):
    new_first = beta_one * moment_one + (1.0 - beta_one) * gradient
    new_second = beta_two * moment_two + (1.0 - beta_two) * gradient * gradient
    first_hat = new_first / (1.0 - beta_one**step_count)
    second_hat = new_second / (1.0 - beta_two**step_count)
    new_master = master - learn_rate * (
        first_hat / (jnp.sqrt(second_hat) + epsilon) + decay_rate * master
    )
    return new_master, new_first, new_second


def cut_up(cols):
    edges = [cols * sum(SHARES[:k]) // sum(SHARES) // 128 * 128 for k in range(len(SHARES))] + [cols]
    return [(a, b - a) for a, b in zip(edges, edges[1:]) if b > a]


def first_block(core, me_f, j, away):
    low, high = me_f & 1, (me_f >> 1) & 1
    return jnp.where(core == 0, j, low ^ away), jnp.where(core == 0, high ^ away, j)


def gathered(g, wanted, cut, rows, nf, ng):
    cols = g.shape[1] // ng
    blocks = g.reshape(nf // 4, 2, 2, rows, g.shape[1])

    def kernel(g_ref, *refs):
        outs, sem = refs[:-1], refs[-1]
        me_f, me_g = lax.axis_index("fsdp"), lax.axis_index("grp")
        moves = []
        for n, (sibling, away) in enumerate(wanted):
            core = (me_g & 1) ^ sibling
            for k, (start, width) in enumerate(cut):
                for j in range(2):
                    low, high = first_block(core, me_f, j, away)
                    for x in range(ng // 2):
                        column = pl.multiple_of((2 * x + core) * cols + start, 128)
                        moves.append(pltpu.make_async_copy(
                            g_ref.at[:, high, low, :, pl.ds(column, width)], outs[n * len(cut) + k].at[j, :, x], sem.at[len(moves)]))
        for m in moves:
            m.start()
        for m in moves:
            m.wait()

    flat = pl.pallas_call(
        kernel,
        out_shape=[jax.ShapeDtypeStruct((2, nf // 4, ng // 2, rows, w), g.dtype) for _ in wanted for _, w in cut],
        in_specs=[ANY],
        out_specs=[VMEM] * (len(wanted) * len(cut)),
        scratch_shapes=[pltpu.SemaphoreType.DMA((ng * len(wanted) * len(cut),))],
        compiler_params=pltpu.CompilerParams(vmem_limit_bytes=LIMIT),
        cost_estimate=pl.CostEstimate(flops=0, bytes_accessed=g.size * len(wanted), transcendentals=0),
    )(blocks)
    return [list(flat[n * len(cut) : (n + 1) * len(cut)]) for n in range(len(wanted))]


def gathered_plain(g, wanted, cut, rows, nf, ng):
    cols = g.shape[1] // ng
    blocks = g.reshape(nf // 4, 2, 2, rows, g.shape[1])
    me_f, me_g = lax.axis_index("fsdp"), lax.axis_index("grp")

    def block(core, away, j, x, start, width):
        low, high = first_block(core, me_f, j, away)
        part = lax.dynamic_slice(blocks, (0, high, low, 0, (2 * x + core) * cols + start), (nf // 4, 1, 1, rows, width))
        return part[:, 0, 0]

    return [
        [jnp.stack([jnp.stack([block((me_g & 1) ^ sibling, away, j, x, a, w) for x in range(ng // 2)], 1) for j in range(2)]) for a, w in cut]
        for sibling, away in wanted
    ]


def finish(own, other, states, near, cols):
    parts, rows = len(own), own[0].shape[1]
    ng = 2 * len(states)
    edges = cut_up(cols)

    def kernel(first, *refs):
        refs = list(refs)
        take = lambda n: [refs.pop(0) for _ in range(n)]
        own = take(parts) if first else []
        other = dict(zip(range(parts - 1) if first else [parts - 1], take(parts - 1 if first else 1)))
        states, near = take(ng // 2) if first else [], take(ng // 2)
        if first:
            outs = take(3)
        else:
            take(4)
        weights, copies = take(1)[0], take(3)
        wide, thin, sem = take(3)
        me = lax.axis_index("grp")
        last = lax.rem(me + ng - 1, ng)
        moves = []

        def move(source, target):
            moves.append(pltpu.make_async_copy(source, target, sem.at[len(moves)]))
            moves[-1].start()

        def block(n, part, state, x, edge, keep):
            start, width = edge
            new = updated(part[x].astype(F32), *[state[i, :, start : start + width] for i in range(3)])
            thin[n, :, start : start + width] = new[0].astype(BF16)
            if keep:
                for i in range(3):
                    wide[i, :, start : start + width] = new[i]

        for k in range(len(states)):
            for part, edge in zip(own, edges):
                block(2 * k, part, states[k], (me >> 1) ^ k, edge, k == 0)
            if k == 0:
                for i in range(3):
                    move(wide.at[i], outs[i])
            move(thin.at[2 * k], weights.at[:, pl.ds(pl.multiple_of((me ^ (2 * k)) * cols, 128), cols)])
        for index, part in other.items():
            start, width = edges[index]
            here = pl.ds(start, width)
            for k in range(ng // 2):
                @pl.when((me ^ last) >> 1 == k)
                def _():
                    new = updated(part[last >> 1].astype(F32), *[near[k][i, :, start : start + width] for i in range(3)])
                    for i in range(3):
                        wide[3 + i, :, start : start + width] = new[i]
            for i in range(3):
                move(wide.at[3 + i, :, here], copies[i].at[:, here])
            for k in range(ng // 2):
                block(2 * k + 1, part, near[k], (me >> 1) ^ k, edges[index], False)
                column = pl.multiple_of((me ^ (2 * k + 1)) * cols + start, 128)
                move(thin.at[2 * k + 1, :, here], weights.at[:, pl.ds(column, width)])
        for m in moves:
            m.wait()

    shape = jax.ShapeDtypeStruct((rows, cols), F32)
    shapes = [jax.ShapeDtypeStruct((rows, cols * ng), BF16)] + [shape] * 3
    scratch = [pltpu.VMEM((6, rows, cols), F32), pltpu.VMEM((ng, rows, cols), BF16)]
    early = pl.pallas_call(
        functools.partial(kernel, True),
        out_shape=[shape] * 3 + shapes,
        in_specs=[VMEM] * (2 * parts - 1 + ng),
        out_specs=[ANY] * 7,
        scratch_shapes=scratch + [pltpu.SemaphoreType.DMA((3 + ng // 2 + (3 + ng // 2) * (parts - 1),))],
        cost_estimate=pl.CostEstimate(flops=40 * rows * cols * ng, bytes_accessed=12 * rows * cols * ng, transcendentals=0),
        compiler_params=pltpu.CompilerParams(vmem_limit_bytes=LIMIT),
    )(*own, *other[:-1], *states, *near)
    late = pl.pallas_call(
        functools.partial(kernel, False),
        out_shape=shapes,
        in_specs=[VMEM] * (1 + ng // 2) + [ANY] * 4,
        out_specs=[ANY] * 4,
        scratch_shapes=scratch + [pltpu.SemaphoreType.DMA((3 + ng // 2,))],
        input_output_aliases={1 + ng // 2 + i: i for i in range(4)},
        compiler_params=pltpu.CompilerParams(vmem_limit_bytes=LIMIT),
    )(other[-1], *near, *early[3:])
    return (*early[:3], *late)


def finish_plain(own, other, states, near, cols):
    me = lax.axis_index("grp")
    own, other = jnp.concatenate(own, -1), jnp.concatenate(other, -1)
    ng = 2 * len(states)
    gradient = jnp.stack([pick((own, other)[r & 1], (me >> 1) ^ (r >> 1), 0) for r in range(ng)])
    state = jnp.stack([(states, near)[r & 1][r >> 1] for r in range(ng)])
    new = updated(gradient.astype(F32), state[:, 0], state[:, 1], state[:, 2])
    blocks = new[0].astype(BF16)
    weights = jnp.zeros((own.shape[1], cols * ng), BF16)
    for r in range(ng):
        weights = lax.dynamic_update_slice(weights, blocks[r], (0, (me ^ r) * cols))
    last = (me + ng - 1) % ng
    return (*[n[0] for n in new], weights, *[pick(n, me ^ last, 0) for n in new])


def onward(t, core, me_f, labels, want):
    a, b = [names.index(w) for names, w in zip(labels, want)]
    bit = [(me_f >> w) & 1 for w in want]

    def choose(j, away):
        if a == b:
            return pick(t, jnp.where(core == 0, bit[0], bit[1]) ^ away, a)
        at = {a: jnp.where(core == 0, bit[0] ^ away, j), b: jnp.where(core == 0, j, bit[1] ^ away)}
        return pick(pick(t, at[max(a, b)], max(a, b)), at[min(a, b)], min(a, b))

    def chosen(away):
        return choose(0, away) if a == b else jnp.stack([choose(j, away) for j in range(2)])

    rest = [[name for i, name in enumerate(names) if i not in (a, b)] for names in labels]
    left = rest if a == b else [[labels[0][b]] + rest[0], [labels[1][a]] + rest[1]]
    return chosen(1).astype(BF16), chosen(0), left


def shards(grads, master, moment_one, moment_two):
    ng, nf = lax.axis_size("grp"), lax.axis_size("fsdp")
    g_bits, f_bits = ng.bit_length() - 1, nf.bit_length() - 1
    me_f, me_g = lax.axis_index("fsdp"), lax.axis_index("grp")
    core = me_g & 1
    g = grads[0, 0]
    rows, cols = g.shape[0] // nf, g.shape[1] // ng
    cut = cut_up(cols)
    local = rows % 16 == 0 and cols % 128 == 0

    gather = gathered if local else gathered_plain
    away_out, away_own = [], []
    for edge in cut:
        (out,), (mine,) = gather(g, [(1, 1), (0, 1)], [edge], rows, nf, ng)
        away_out.append(out)
        away_own.append(mine)
    split = lambda t: t.reshape((2,) * (f_bits - 1) + t.shape[2:])
    got_away = [split(swap(t, [1, 1])) for t in away_out]
    sent = [(split(t).astype(F32) + x.astype(F32)).astype(BF16) for t, x in zip(away_own, got_away)]
    later = lax.optimization_barrier((g, sent[-1]))[0]
    kept_out, kept_own = gather(later, [(1, 0), (0, 0)], cut, rows, nf, ng)
    got_kept = [split(swap(t, [1, 1])) for t in kept_out]
    kept = [split(t).astype(F32) + x.astype(F32) for t, x in zip(kept_own, got_kept)]

    high = list(range(f_bits - 1, 1, -1))
    labels = [[[0] + high, [1] + high] for _ in cut]
    orders = [o + list(range(len(o), f_bits)) for o in ORDERS]
    for step in range(f_bits):
        masks = [ng << o[step] for o in orders]
        if step == 0:
            held = lax.optimization_barrier(((master, moment_one, moment_two), sent[-1]))[0]
            states = [jnp.stack(held)]
            for b in range(1, g_bits):
                states = states + [swap(s, [1 << b] * 2) for s in states]
        got = [swap(s, masks) for s in sent]
        ts = [k + x.astype(F32) for k, x in zip(kept, got)]
        if step == f_bits - 1:
            break
        want = [o[step + 1] for o in orders]
        moved = [onward(t, core, me_f, names, want) for t, names in zip(ts, labels)]
        sent, kept, labels = [list(m) for m in zip(*moved)]

    for b in range(1, g_bits):
        rounded = [t.astype(BF16) for t in ts]
        if b == g_bits - 1:
            states = lax.optimization_barrier((states, rounded[-1]))[0]
            near = [swap(s, [1, 1]) for s in states]
        got = [swap(t, [1 << b] * 2) for t in rounded]
        ts = [t.astype(F32) + x.astype(F32) for t, x in zip(rounded, got)]
    own = [(t / (ng * nf)).astype(BF16) for t in ts]
    other = [swap(t, [1, 1]) for t in own]
    return (finish if local else finish_plain)(own, other, states, near, cols)


def solution(mesh):
    return jax.shard_map(
        shards,
        mesh=mesh,
        in_specs=(P("grp", "fsdp", None, None), P("fsdp", "grp"), P("fsdp", "grp"), P("fsdp", "grp")),
        out_specs=(P("fsdp", "grp"), P("fsdp", "grp"), P("fsdp", "grp"), P("fsdp", None), P("fsdp", "grp"), P("fsdp", "grp"), P("fsdp", "grp")),
        check_vma=False,
    )
```
